256 devices in a mesh: dp: 4 (over z_lo), text: 8 (over y, core), image: 8 (over x, z_hi).
Axes of the slice: x: 4, y: 4, z: 8 (z_hi: 2, z_lo: 4; z = z_hi * 4 + z_lo), core: 2. Of those that a mesh axis runs over, the one named last changes fastest.
Arguments:
- tokens: bfloat16 [32768, 4096], P(('dp', 'text', 'image')), may hold values from -24 to 24
- modality: int32 [32768], P(('dp', 'text', 'image')), may hold values from 0 to 1, as said below
- gain_text: float32 [4096], replicated, may hold values from 0.1 to 1.9
- gain_image: float32 [4096], replicated, may hold values from 0.1 to 1.9
- text_weight: bfloat16 [4096, 4096], P(('dp', 'image'), 'text'), may hold values from -0.0234375 to 0.0234375
- image_weight: bfloat16 [4096, 4096], P(('dp', 'text'), 'image'), may hold values from -0.0234375 to 0.0234375
- cotangent: bfloat16 [32768, 4096], P(('dp', 'text', 'image')), may hold values from -3 to 3
Outputs:
- queries: bfloat16 [32768, 4096], P(('dp', 'text', 'image'))
- token_grads: bfloat16 [32768, 4096], P(('dp', 'text', 'image'))
- text_weight_grad: float32 [4096, 4096], P(('dp', 'image'), 'text')
- image_weight_grad: float32 [4096, 4096], P(('dp', 'text'), 'image')
- text_gain_grad: float32 [4096], replicated
- image_gain_grad: float32 [4096], replicated
The draws below stay inside these ranges and needn't reach their ends.
Inputs may be any that keep to these rules, and one draw needn't show every extreme that they name: `modality`: entry 0 marks a text token and 1 an image token. In each aligned block of 128 positions at most 72 entries are 0 and at most 72 are 1; both bounds are met with equality in some blocks of every draw.
All inputs are finite; a program needn't handle non-finite values.
Results may differ from the reference program's by a relative error of at most 0.018.
Values may be sent and summed in bfloat16 or wider, within the bound.
A program may use at most 128 MiB of HBM per device.

```python
from functools import partial
import jax
import jax.numpy as jnp
from jax import lax

D = 4096
E = 4096
TOK_DEV = 128
CAP = 72
DP_DEVS = 4
TEXT_DEVS = 8
IMAGE_DEVS = 8
TOKENS = 32768


def draw_modality(key, part):
    key = jax.random.fold_in(key, 7)
    key_list = jax.random.split(key, 6)
    grid_shape = (DP_DEVS, TEXT_DEVS, IMAGE_DEVS)
    low_count = TOK_DEV - CAP
    counts = jax.random.randint(key_list[0], grid_shape, low_count, CAP + 1)
    dp_full = jax.random.randint(key_list[1], (), 0, DP_DEVS)
    image_full = jax.random.randint(key_list[2], (), 0, IMAGE_DEVS)
    text_full = jax.random.randint(key_list[3], (), 0, TEXT_DEVS)
    dp_other = (dp_full + 1 + jax.random.randint(key_list[4], (), 0, DP_DEVS - 1)) % DP_DEVS
    dp_grid = lax.broadcasted_iota(jnp.int32, grid_shape, 0)
    text_grid = lax.broadcasted_iota(jnp.int32, grid_shape, 1)
    image_grid = lax.broadcasted_iota(jnp.int32, grid_shape, 2)
    counts = jnp.where((dp_grid == dp_full) & (image_grid == image_full), CAP, counts)
    counts = jnp.where((dp_grid == dp_other) & (text_grid == text_full), low_count, counts)
    flat_counts = counts.reshape(-1)
    positions = lax.broadcasted_iota(jnp.int32, (flat_counts.shape[0], TOK_DEV), 1)
    scores = jax.random.randint(key_list[5], (flat_counts.shape[0], TOK_DEV), 0, 1 << 20) * TOK_DEV + positions
    ranks = jnp.argsort(jnp.argsort(scores, axis=1), axis=1)
    return (ranks >= flat_counts[:, None]).astype(jnp.int32).reshape(TOKENS)


def spiked(values, key, source, target, blocks, factor):
    owner, partner = [(jnp.arange(values.shape[dim]) // (values.shape[dim] // blocks)).reshape([-1 if axis == dim else 1 for axis in range(values.ndim)]) for dim in (source, target)]
    chosen = jax.random.permutation(key, blocks)[partner]
    strong = (owner == chosen) | (owner == (partner + blocks // 2) % blocks)
    return jnp.where(strong, factor * values, values)


def block_levels(key, extent, cuts, least, largest):
    factor_of, own = 1.0, jax.random.fold_in(key, 6)
    for axis_at, blocks in cuts:
        draws = jnp.exp(jax.random.uniform(jax.random.fold_in(own, axis_at), (blocks,), jnp.float32, least / len(cuts), largest / len(cuts)))
        factor_of = factor_of * jnp.repeat(draws, extent[axis_at] // blocks).reshape([-1 if axis == axis_at else 1 for axis in range(len(extent))])
    return factor_of


def scatter_about(rng, shape, deviation, most, cuts=(), kind=jnp.bfloat16):
    gain = block_levels(rng, shape, cuts, -0.22, 0.18) if cuts else 1.0
    result = jax.random.normal(rng, shape, jnp.float32) * deviation * gain
    return jnp.minimum(jnp.maximum(result, -most), most).astype(kind)


def bell_draw_with(key, shape, width, bound, cuts, heavy, kind=jnp.bfloat16):
    result = width * jax.random.normal(key, shape, jnp.float32)
    if cuts:
        result = result * block_levels(key, shape, cuts, -0.22, 0.18)
    return jnp.clip(spiked(result, jax.random.fold_in(key, 3), *heavy), -bound, bound).astype(kind)


def setup_inputs(seed: int = 0) -> dict:
    keys = jax.random.split(jax.random.key(seed), 8)
    return {
        "tokens": bell_draw_with(keys[0], (TOKENS, D), 1.0, 24.0, ((0, 256),), (0, 1, 256, 6.0)),
        "modality": draw_modality(jax.random.fold_in(keys[7], 71), 0),
        "gain_text": jnp.clip(1.0 + 0.18 * jax.random.normal(keys[2], (D,), jnp.float32), 0.1, 1.9),
        "gain_image": jnp.clip(1.0 + 0.18 * jax.random.normal(keys[3], (D,), jnp.float32), 0.1, 1.9),
        "text_weight": scatter_about(keys[4], (D, E), (16 * D) ** -0.5, 0.0234375, ((0, 32), (1, 8))),
        "image_weight": scatter_about(keys[5], (D, E), (16 * D) ** -0.5, 0.0234375, ((0, 32), (1, 8))),
        "cotangent": scatter_about(keys[6], (TOKENS, E), 0.5, 3.0, ((0, 256),)),
    }


EPSILON = 1e-05

def project(block_count, inputs, upstream, weight):
    outputs = jnp.dot(inputs, weight, preferred_element_type=jnp.float32)
    column_span = weight.shape[1] // block_count
    summed = jnp.zeros((inputs.shape[0], weight.shape[0]), jnp.float32)
    for block_id in range(block_count):
        first_col = block_id * column_span
        block_term = jnp.dot(upstream[:, first_col:first_col + column_span], weight[:, first_col:first_col + column_span].T, preferred_element_type=jnp.float32)
        summed = summed + lax.optimization_barrier(block_term.astype(jnp.bfloat16)).astype(jnp.float32)
    weight_grad = lax.dot_general(inputs, upstream, (((0,), (0,)), ((), ())), preferred_element_type=jnp.float32)
    return (outputs, summed, weight_grad)

def skip_block(block_count, inputs, upstream, weight):
    return (jnp.zeros((inputs.shape[0], weight.shape[1]), jnp.float32), jnp.zeros((inputs.shape[0], weight.shape[0]), jnp.float32), jnp.zeros(weight.shape, jnp.float32))

def reference(tokens, modality, gain_text, gain_image, text_weight, image_weight, cotangent):
    total_rows = tokens.shape[0]
    block_rows = 512
    block_total = total_rows // block_rows
    sorted_ids = jnp.argsort(modality, stable=True).astype(jnp.int32)

    def step(running, block_index):
        text_acc, image_acc, text_gsum, image_gsum = running
        row_ids = lax.dynamic_slice_in_dim(sorted_ids, block_index * block_rows, block_rows)
        as_float = tokens[row_ids].astype(jnp.float32)
        is_text = modality[row_ids] == 0
        inv_rms = lax.rsqrt(lax.optimization_barrier(jnp.mean(as_float * as_float, axis=1)) + EPSILON)
        unit_rows = as_float * inv_rms[:, None]
        row_gains = jnp.where(is_text[:, None], gain_text[None, :], gain_image[None, :])
        normed = (unit_rows * row_gains).astype(jnp.bfloat16)
        upstream = cotangent[row_ids]
        text_in = jnp.where(is_text[:, None], normed, jnp.zeros_like(normed))
        image_in = jnp.where(is_text[:, None], jnp.zeros_like(normed), normed)
        text_out, text_back, text_dw = lax.cond(jnp.any(is_text), partial(project, TEXT_DEVS), partial(skip_block, TEXT_DEVS), text_in, upstream, text_weight)
        image_out, image_back, image_dw = lax.cond(jnp.any(jnp.logical_not(is_text)), partial(project, IMAGE_DEVS), partial(skip_block, IMAGE_DEVS), image_in, upstream, image_weight)
        queries = jnp.where(is_text[:, None], text_out, image_out).astype(jnp.bfloat16)
        normed_grad = jnp.where(is_text[:, None], text_back, image_back)
        scaled_grad = normed_grad * row_gains
        along_unit = lax.optimization_barrier(jnp.mean(scaled_grad * unit_rows, axis=1))
        token_grads = (inv_rms[:, None] * (scaled_grad - unit_rows * along_unit[:, None])).astype(jnp.bfloat16)
        gain_term = normed_grad * unit_rows
        text_gsum = text_gsum + lax.optimization_barrier(jnp.sum(jnp.where(is_text[:, None], gain_term, 0.0), axis=0))
        image_gsum = image_gsum + lax.optimization_barrier(jnp.sum(jnp.where(is_text[:, None], 0.0, gain_term), axis=0))
        return ((text_acc + text_dw, image_acc + image_dw, text_gsum, image_gsum), (queries, token_grads))
    start_state = (jnp.zeros(text_weight.shape, jnp.float32), jnp.zeros(image_weight.shape, jnp.float32), jnp.zeros(gain_text.shape, jnp.float32), jnp.zeros(gain_image.shape, jnp.float32))
    final_state, stacked = lax.scan(step, start_state, jnp.arange(block_total, dtype=jnp.int32))
    inverse_ids = jnp.argsort(sorted_ids).astype(jnp.int32)
    queries = stacked[0].reshape(total_rows, -1)[inverse_ids]
    token_grads = stacked[1].reshape(total_rows, -1)[inverse_ids]
    return (queries, token_grads, final_state[0], final_state[1], final_state[2], final_state[3])
```

```python
import functools

import jax
import jax.numpy as jnp
from jax import lax
from jax.experimental import pallas as pl
from jax.experimental.pallas import tpu as pltpu
from jax.sharding import PartitionSpec as P

MESH = pl.DeviceIdType.MESH
CAP = 72
EPSILON = 1e-05
F32 = jnp.float32
BF16 = jnp.bfloat16


def dot_nn(left, right):
    return jnp.dot(left, right, preferred_element_type=F32)


def dot_nt(left, right):
    return lax.dot_general(left, right, (((1,), (1,)), ((), ())), preferred_element_type=F32)


def dot_tn(left, right):
    return lax.dot_general(left, right, (((0,), (0,)), ((), ())), preferred_element_type=F32)


def layer(
    dims,
    mod_ref, gt_ref, gi_ref, tok_ref, cot_ref, wt_ref, wi_ref,
    q_out, tg_out, dwt_out, dwi_out, ggt_out, ggi_out,
    pick, place, flag, inv, work, gacc,
    xs, gs, xall, gall, w, qp, dp, qr, dr, qf, df,
    dw_own, dw_peer, dw_sum, dw_z,
    g_core, g_b, g_z, g_c,
    send, x1, x2, g1, g2, w1, w2, q1, q2, d1, d2, e1, e2, s1, s2, s3, s4,
):
    S, ZL, T, R, DS, ES = dims
    NZ = 2 * ZL
    CH = DS // ZL
    WR, WC = CH // 2, ES // 2
    D, E = DS * S, ES * S
    GR = DS // 128
    zl, text, image = lax.axis_index("dp"), lax.axis_index("text"), lax.axis_index("image")
    y, core = lax.div(text, 2), lax.rem(text, 2)
    x, zh = lax.div(image, 2), lax.rem(image, 2)
    z = zh * ZL + zl

    def cc(m):
        return x + (y - x) * m

    def bc(m):
        return y + (x - y) * m

    def along_c(m, k):
        return (zl, lax.rem(text + 2 * k * m, 2 * S), lax.rem(image + 2 * k * (1 - m), 2 * S))

    def along_b(m, k):
        return (zl, lax.rem(text + 2 * k * (1 - m), 2 * S), lax.rem(image + 2 * k * m, 2 * S))

    def along_z(k):
        to = lax.rem(z + k, NZ)
        return (lax.rem(to, ZL), text, 2 * x + lax.div(to, ZL))

    partner = (zl, text + 1 - 2 * core, image)

    def push(src, dst, send_sem, recv_sem, device):
        return pltpu.make_async_remote_copy(
            src_ref=src, dst_ref=dst, send_sem=send_sem, recv_sem=recv_sem,
            device_id=device, device_id_type=MESH,
        )

    def arrived(dst, recv_sem):
        push(dst, dst, send.at[0], recv_sem, partner).wait_recv()

    def sent(src, send_sem):
        push(src, src, send_sem, x1.at[0], partner).wait_send()

    barrier = pltpu.get_barrier_semaphore()

    @pl.loop(1, S)
    def _(k):
        pl.semaphore_signal(barrier, inc=1, device_id=along_c(0, k), device_id_type=MESH)
        pl.semaphore_signal(barrier, inc=1, device_id=along_b(0, k), device_id_type=MESH)

    @pl.loop(1, NZ)
    def _(k):
        pl.semaphore_signal(barrier, inc=1, device_id=along_z(k), device_id_type=MESH)

    pl.semaphore_signal(barrier, inc=1, device_id=partner, device_id_type=MESH)

    rows = lax.broadcasted_iota(jnp.int32, (T, T), 0)
    cols = lax.broadcasted_iota(jnp.int32, (T, T), 1)
    flag_row = jnp.where(mod_ref[...] == 0, 1.0, 0.0)
    wide = jnp.broadcast_to(flag_row, (T, T))
    flag_col = jnp.sum(jnp.where(rows == cols, wide, 0.0), axis=1, keepdims=True)
    rank_col = jnp.sum(jnp.where(cols < rows, wide, 0.0), axis=1, keepdims=True)
    tall = jnp.broadcast_to(flag_col, (T, T))
    rank_row = jnp.sum(jnp.where(rows < cols, tall, 0.0), axis=0, keepdims=True)
    flag[...] = flag_col
    slot = lax.broadcasted_iota(jnp.int32, (R, T), 0).astype(F32)
    spot = lax.broadcasted_iota(jnp.int32, (R, T), 1).astype(F32)
    pick[0] = jnp.where((rank_row == slot) & (flag_row > 0.5), 1.0, 0.0).astype(BF16)
    pick[1] = jnp.where((spot - rank_row == slot) & (flag_row < 0.5), 1.0, 0.0).astype(BF16)
    slot = lax.broadcasted_iota(jnp.int32, (T, R), 1).astype(F32)
    spot = lax.broadcasted_iota(jnp.int32, (T, R), 0).astype(F32)
    place[0] = jnp.where((rank_col == slot) & (flag_col > 0.5), 1.0, 0.0).astype(BF16)
    place[1] = jnp.where((spot - rank_col == slot) & (flag_col < 0.5), 1.0, 0.0).astype(BF16)

    def w_at(m, from_z, from_core):
        from_zh, from_zl = lax.div(from_z, ZL), lax.rem(from_z, ZL)
        half = from_core + (from_zh - from_core) * m
        row = 2 * from_zl + from_zh + (from_core - from_zh) * m
        return w.at[m * 2 + half, pl.ds(pl.multiple_of(row * WR, WR), WR), :]

    w_at(0, z, core)[...] = wt_ref[...]
    w_at(1, z, core)[...] = wi_ref[...]

    pl.semaphore_wait(barrier, 2 * (S - 1) + NZ)

    @pl.loop(0, 2)
    def _(m):
        mine = w_at(m, z, core)
        push(mine, mine, send.at[17 + m], w2.at[m * NZ], partner).start()

        @pl.loop(1, NZ)
        def _(k):
            push(mine, mine, send.at[17 + m], w1.at[m * NZ + k], along_z(k)).start()

    @pl.loop(0, 2 * S)
    def _(i):
        m, b = lax.div(i, S), lax.rem(i, S)
        part = cot_ref[:, pl.ds(pl.multiple_of(b * ES, ES), ES)]
        gs[i] = dot_nn(pick[m], part).astype(BF16)

    @pl.loop(0, 2)
    def _(m):
        mine = (m * S + bc(m)) * S + cc(m)
        gall[mine] = gs[m * S + bc(m)]

        @pl.loop(1, S)
        def _(j):
            to = lax.rem(bc(m) + j, S)
            push(gs.at[m * S + to], gall.at[mine], send.at[2], g1.at[m * S + j], along_b(m, j)).start()

        @pl.loop(1, S)
        def _(k):
            push(
                gall.at[mine], gall.at[mine], send.at[3], g2.at[m * S * S + k], along_c(m, k)
            ).start()

    squares = jnp.zeros((T, CH), F32)
    for i in range(S * ZL):
        part = tok_ref[:, i * CH:(i + 1) * CH].astype(F32)
        squares = squares + part * part
    inv_rms = lax.rsqrt(jnp.sum(squares, axis=1, keepdims=True) / D + EPSILON)
    inv[...] = inv_rms

    @pl.loop(0, S * ZL)
    def _(i):
        c, zq = lax.div(i, ZL), lax.rem(i, ZL)
        at = pl.ds(pl.multiple_of(zq * (S * CH) + c * CH, CH), CH)
        to = pl.ds(pl.multiple_of(zq * CH, CH), CH)
        unit = tok_ref[:, at].astype(F32) * inv[...]
        gains = jnp.where(flag[...] > 0.5, gt_ref[:, at], gi_ref[:, at])
        normed = (unit * gains).astype(BF16)
        xs[c, :, to] = dot_nn(pick[0], normed).astype(BF16)
        xs[S + c, :, to] = dot_nn(pick[1], normed).astype(BF16)

    @pl.loop(0, 2)
    def _(m):
        mine = (m * S + bc(m)) * S + cc(m)
        xall[mine] = xs[m * S + cc(m)]

        @pl.loop(1, S)
        def _(k):
            to = lax.rem(cc(m) + k, S)
            push(xs.at[m * S + to], xall.at[mine], send.at[4], x1.at[m * S + k], along_c(m, k)).start()

        @pl.loop(1, S)
        def _(j):
            push(
                xall.at[mine], xall.at[mine], send.at[5], x2.at[m * S * S + j * S], along_b(m, j)
            ).start()

    @pl.loop(1, S)
    def _(j):
        @pl.loop(0, 2)
        def _(m):
            block = gall.at[(m * S + lax.rem(bc(m) + S - j, S)) * S + cc(m)]
            arrived(block, g1.at[m * S + j])

            @pl.loop(1, S)
            def _(k):
                push(block, block, send.at[3], g2.at[(m * S + j) * S + k], along_c(m, k)).start()

    @pl.loop(1, S)
    def _(k):
        @pl.loop(0, 2)
        def _(m):
            block = xall.at[(m * S + bc(m)) * S + lax.rem(cc(m) + S - k, S)]
            arrived(block, x1.at[m * S + k])

            @pl.loop(1, S)
            def _(j):
                push(block, block, send.at[5], x2.at[(m * S + j) * S + k], along_b(m, j)).start()

    @pl.loop(1, NZ)
    def _(k):
        @pl.loop(0, 2)
        def _(m):
            block = w_at(m, lax.rem(z + NZ - k, NZ), core)
            arrived(block, w1.at[m * NZ + k])
            push(block, block, send.at[19 + m], w2.at[m * NZ + k], partner).start()

    @pl.loop(0, NZ)
    def _(k):
        @pl.loop(0, 2)
        def _(m):
            arrived(w_at(m, lax.rem(z + NZ - k, NZ), 1 - core), w2.at[m * NZ + k])

    @pl.loop(0, 2)
    def _(m):
        @pl.loop(0, S)
        def _(j):
            b = lax.rem(bc(m) + S - j, S)
            base = (m * S + b) * S

            @pl.when(j > 0)
            def _():
                @pl.loop(0, S)
                def _(k):
                    c = lax.rem(cc(m) + S - k, S)
                    arrived(xall.at[base + c], x2.at[(m * S + j) * S + k])

            block = xall[pl.ds(base, S)].reshape(S * R, DS)
            for half in range(2):
                part = dot_nn(block, w[m * 2 + half]).astype(BF16)
                qp[pl.ds(base, S), :, half * WC:(half + 1) * WC] = part.reshape(S, R, WC)

            @pl.loop(1, S)
            def _(k):
                c = lax.rem(cc(m) + k, S)
                at = (m * (S - 1) + k - 1) * S + b
                push(
                    qp.at[base + c], qr.at[at], send.at[7], q1.at[(m * S + k) * S + b], along_c(m, k)
                ).start()

    gacc[...] = jnp.zeros_like(gacc)

    @pl.loop(0, 2)
    def _(m):
        @pl.loop(1, S)
        def _(k):
            c = lax.rem(cc(m) + S - k, S)

            @pl.loop(0, S)
            def _(j):
                b = lax.rem(bc(m) + S - j, S)
                arrived(gall.at[(m * S + b) * S + c], g2.at[(m * S + j) * S + k])

        @pl.loop(1, S + 1)
        def _(j):
            b = lax.rem(bc(m) + j, S)
            base = (m * S + b) * S
            for part in range(2):
                at = slice(part * (DS // 2), (part + 1) * (DS // 2))
                total = dot_nt(
                    gall[pl.ds(base, S), :, :WC].reshape(S * R, WC), w[m * 2, at, :]
                ) + dot_nt(
                    gall[pl.ds(base, S), :, WC:].reshape(S * R, WC), w[m * 2 + 1, at, :]
                )
                dp[pl.ds(base, S), :, at] = total.astype(BF16).reshape(S, R, DS // 2)
                rowed = xall[pl.ds(base, S), :, at].reshape(S * R, DS // 2).astype(F32)
                gacc[m, :, at] += jnp.sum(total * rowed, axis=0, keepdims=True)

            @pl.when(j < S)
            def _():
                push(
                    dp.at[pl.ds(base, S)], dr.at[pl.ds((m * (S - 1) + j - 1) * S, S)],
                    send.at[8], d1.at[m * S + j], along_b(m, j),
                ).start()

        for i in range(GR):
            g_core[m * 2 + core, i:i + 1, :] = gacc[m, :, i * 128:(i + 1) * 128]
        mine = g_core.at[m * 2 + core]
        push(mine, mine, send.at[9], s1.at[m], partner).start()

    def weight_grad(m):
        @pl.loop(0, ZL)
        def _(zq):
            at = pl.ds(pl.multiple_of(zq * CH, CH), CH)
            left = xall[pl.ds(m * S * S, S * S), :, at].reshape(S * S * R, CH)
            for half in range(2):
                right = gall[pl.ds(m * S * S, S * S), :, half * WC:(half + 1) * WC]
                work[:, half * WC:(half + 1) * WC] = dot_tn(left, right.reshape(S * S * R, WC))
            upper, lower = work[:WR, :WC], work[WR:, WC:]
            cross = (work[:WR, WC:], work[WR:, :WC])
            first = jnp.where(m == 0, cross[0], cross[1])
            second = jnp.where(m == 0, cross[1], cross[0])
            low = core == 0
            dw_own[m * NZ + zq] = jnp.where(low, upper, first)
            dw_own[m * NZ + ZL + zq] = jnp.where(low, second, lower)
            dw_peer[m * NZ + zq] = jnp.where(low, first, upper).astype(BF16)
            dw_peer[m * NZ + ZL + zq] = jnp.where(low, lower, second).astype(BF16)
            for part in range(2):
                at = m * NZ + part * ZL + zq
                push(dw_peer.at[at], dw_sum.at[at], send.at[10], e1.at[at], partner).start()

    def weight_shares(m):
        @pl.loop(1, NZ + 1)
        def _(k):
            to = lax.rem(z + k, NZ)
            at = m * NZ + to
            arrived(dw_sum.at[at], e1.at[at])
            total = dw_own[at] + dw_sum[at].astype(F32)
            dw_own[at] = total

            @pl.when(k < NZ)
            def _():
                dw_sum[at] = total.astype(BF16)
                push(
                    dw_sum.at[at], dw_z.at[m * (NZ - 1) + k - 1], send.at[11],
                    e2.at[m * NZ + k], along_z(k),
                ).start()

    def gain_step(m, came, slots, going, place_at):
        total = came[m * slots]
        for i in range(1, slots):
            total = total + came[m * slots + i]
        going[place_at] = total

    def gains_b():
        @pl.loop(0, 2)
        def _(m):
            arrived(g_core.at[m * 2 + 1 - core], s1.at[m])
            gain_step(m, g_core, 2, g_b, m * S + bc(m))
            mine = g_b.at[m * S + bc(m)]

            @pl.loop(1, S)
            def _(j):
                push(mine, mine, send.at[12], s2.at[m * S + j], along_b(m, j)).start()

    def gains_z():
        @pl.loop(0, 2)
        def _(m):
            @pl.loop(1, S)
            def _(j):
                arrived(g_b.at[m * S + lax.rem(bc(m) + S - j, S)], s2.at[m * S + j])

            gain_step(m, g_b, S, g_z, m * NZ + z)
            mine = g_z.at[m * NZ + z]

            @pl.loop(1, NZ)
            def _(k):
                push(mine, mine, send.at[13], s3.at[m * NZ + k], along_z(k)).start()

    def gains_c():
        @pl.loop(0, 2)
        def _(m):
            @pl.loop(1, NZ)
            def _(k):
                arrived(g_z.at[m * NZ + lax.rem(z + NZ - k, NZ)], s3.at[m * NZ + k])

            gain_step(m, g_z, NZ, g_c, m * S + cc(m))
            mine = g_c.at[m * S + cc(m)]

            @pl.loop(1, S)
            def _(k):
                push(mine, mine, send.at[14], s4.at[m * S + k], along_c(m, k)).start()

    @pl.loop(0, 2)
    def _(m):
        weight_grad(m)

    gains_b()

    @pl.loop(0, 2)
    def _(m):
        weight_shares(m)

    @pl.loop(0, 2)
    def _(m):
        @pl.loop(1, S + 1)
        def _(j):
            b = lax.rem(bc(m) + j, S)
            mine = (m * S + b) * S + cc(m)
            total = qp[mine].astype(F32)
            for k in range(1, S):
                at = (m * (S - 1) + k - 1) * S + b
                arrived(qr.at[at], q1.at[(m * S + k) * S + b])
                total = total + qr[at].astype(F32)
            qp[mine] = total.astype(BF16)

            @pl.when(j < S)
            def _():
                push(
                    qp.at[mine], qf.at[m * S + bc(m)], send.at[15], q2.at[m * S + j], along_b(m, j)
                ).start()

            @pl.when(j == S)
            def _():
                qf[m * S + bc(m)] = qp[mine]

    gains_z()

    @pl.loop(0, 2)
    def _(m):
        @pl.loop(1, S)
        def _(j):
            arrived(dr.at[pl.ds((m * (S - 1) + j - 1) * S, S)], d1.at[m * S + j])

        @pl.loop(1, S + 1)
        def _(k):
            c = lax.rem(cc(m) + k, S)
            mine = (m * S + bc(m)) * S + c
            total = dp[mine].astype(F32)
            for j in range(1, S):
                total = total + dr[(m * (S - 1) + j - 1) * S + c].astype(F32)
            dp[mine] = total.astype(BF16)

            @pl.when(k < S)
            def _():
                push(
                    dp.at[mine], df.at[m * S + cc(m)], send.at[16], d2.at[m * S + k], along_c(m, k)
                ).start()

            @pl.when(k == S)
            def _():
                df[m * S + cc(m)] = dp[mine]

    gains_c()

    @pl.loop(0, 2)
    def _(m):
        @pl.loop(1, S)
        def _(j):
            arrived(qf.at[m * S + lax.rem(bc(m) + S - j, S)], q2.at[m * S + j])

    @pl.loop(0, S)
    def _(b):
        both = dot_nn(place[0], qf[b]) + dot_nn(place[1], qf[S + b])
        q_out[:, pl.ds(pl.multiple_of(b * ES, ES), ES)] = both.astype(BF16)

    @pl.loop(0, 2)
    def _(m):
        @pl.loop(1, S)
        def _(k):
            arrived(df.at[m * S + lax.rem(cc(m) + S - k, S)], d2.at[m * S + k])

    def columns(i):
        c, zq = lax.div(i, ZL), lax.rem(i, ZL)
        at = pl.ds(pl.multiple_of(zq * (S * CH) + c * CH, CH), CH)
        return c, pl.ds(pl.multiple_of(zq * CH, CH), CH), at

    def scaled(i, along):
        c, local, at = columns(i)
        normed_grad = dot_nn(place[0], df[c, :, local]) + dot_nn(place[1], df[S + c, :, local])
        gains = jnp.where(flag[...] > 0.5, gt_ref[:, at], gi_ref[:, at])
        return normed_grad * gains, tok_ref[:, at].astype(F32) * inv[...], at

    def dots(i, along):
        grads, unit, _ = scaled(i, along)
        return along + jnp.sum(grads * unit, axis=1, keepdims=True)

    along = lax.fori_loop(0, S * ZL, dots, jnp.zeros((T, 1), F32)) / D

    @pl.loop(0, S * ZL)
    def _(i):
        grads, unit, at = scaled(i, along)
        tg_out[:, at] = (inv[...] * (grads - unit * along)).astype(BF16)

    for m, out in ((0, dwt_out), (1, dwi_out)):
        total = dw_own[m * NZ + z]
        for k in range(1, NZ):
            at = m * (NZ - 1) + k - 1
            arrived(dw_z.at[at], e2.at[m * NZ + k])
            total = total + dw_z[at].astype(F32)
        out[...] = total

    for m, out, gain in ((0, ggt_out, gt_ref), (1, ggi_out, gi_ref)):
        @pl.loop(1, S)
        def _(k):
            arrived(g_c.at[m * S + lax.rem(cc(m) + S - k, S)], s4.at[m * S + k])

        for c in range(S):
            for i in range(GR):
                zq, off = (i * 128) // CH, (i * 128) % CH
                at = slice(zq * S * CH + c * CH + off, zq * S * CH + c * CH + off + 128)
                out[:, at] = g_c[m * S + c, i:i + 1, :] / gain[:, at]

    for m in range(2):
        sent(w.at[2 * m], send.at[17 + m])
        sent(w.at[2 * m + 1, pl.ds(0, (NZ - 1) * WR), :], send.at[19 + m])
    sent(gs.at[pl.ds(0, 2 * (S - 1))], send.at[2])
    sent(gall.at[pl.ds(0, 2 * S * (S - 1))], send.at[3])
    sent(xs.at[pl.ds(0, 2 * (S - 1))], send.at[4])
    sent(xall.at[pl.ds(0, 2 * S * (S - 1))], send.at[5])
    sent(qp.at[pl.ds(0, 2 * S * (S - 1))], send.at[7])
    sent(dp.at[pl.ds(0, 2 * S * (S - 1))], send.at[8])
    sent(g_core.at[pl.ds(0, 2)], send.at[9])
    sent(dw_peer, send.at[10])
    sent(dw_sum.at[pl.ds(0, 2 * (NZ - 1))], send.at[11])
    sent(g_b.at[pl.ds(0, 2 * (S - 1))], send.at[12])
    sent(g_z.at[pl.ds(0, 2 * (NZ - 1))], send.at[13])
    sent(g_c.at[pl.ds(0, 2 * (S - 1))], send.at[14])
    sent(qp.at[pl.ds(0, 2 * (S - 1))], send.at[15])
    sent(dp.at[pl.ds(0, 2 * (S - 1))], send.at[16])


def solution(mesh):
    ZL, S = mesh.shape["dp"], mesh.shape["text"] // 2
    NZ = 2 * ZL

    def shards(tokens, modality, gain_text, gain_image, text_weight, image_weight, cotangent):
        T, D = tokens.shape
        E = cotangent.shape[1]
        R = -(-min(CAP, T) // 16) * 16
        DS, ES = D // S, E // S
        CH = DS // ZL
        WR, WC = CH // 2, ES // 2
        GR = DS // 128
        vmem = pl.BlockSpec(memory_space=pltpu.VMEM)
        dma = pltpu.SemaphoreType.DMA
        outs = pl.pallas_call(
            functools.partial(layer, (S, ZL, T, R, DS, ES)),
            out_shape=(
                jax.ShapeDtypeStruct((T, E), BF16),
                jax.ShapeDtypeStruct((T, D), BF16),
                jax.ShapeDtypeStruct((WR, WC), F32),
                jax.ShapeDtypeStruct((WR, WC), F32),
                jax.ShapeDtypeStruct((1, D), F32),
                jax.ShapeDtypeStruct((1, D), F32),
            ),
            in_specs=[vmem] * 7,
            out_specs=(vmem,) * 6,
            scratch_shapes=[
                pltpu.VMEM((2, R, T), BF16),
                pltpu.VMEM((2, T, R), BF16),
                pltpu.VMEM((T, 1), F32),
                pltpu.VMEM((T, 1), F32),
                pltpu.VMEM((CH, ES), F32),
                pltpu.VMEM((2, 1, DS), F32),
                pltpu.VMEM((2 * S, R, DS), BF16),
                pltpu.VMEM((2 * S, R, ES), BF16),
                pltpu.VMEM((2 * S * S, R, DS), BF16),
                pltpu.VMEM((2 * S * S, R, ES), BF16),
                pltpu.VMEM((4, DS, WC), BF16),
                pltpu.VMEM((2 * S * S, R, ES), BF16),
                pltpu.VMEM((2 * S * S, R, DS), BF16),
                pltpu.VMEM((2 * (S - 1) * S, R, ES), BF16),
                pltpu.VMEM((2 * (S - 1) * S, R, DS), BF16),
                pltpu.VMEM((2 * S, R, ES), BF16),
                pltpu.VMEM((2 * S, R, DS), BF16),
                pltpu.VMEM((2 * NZ, WR, WC), F32),
                pltpu.VMEM((2 * NZ, WR, WC), BF16),
                pltpu.VMEM((2 * NZ, WR, WC), BF16),
                pltpu.VMEM((2 * (NZ - 1), WR, WC), BF16),
                pltpu.VMEM((4, GR, 128), F32),
                pltpu.VMEM((2 * S, GR, 128), F32),
                pltpu.VMEM((2 * NZ, GR, 128), F32),
                pltpu.VMEM((2 * S, GR, 128), F32),
                dma((21,)),
                dma((2 * S,)),
                dma((2 * S * S,)),
                dma((2 * S,)),
                dma((2 * S * S,)),
                dma((2 * NZ,)),
                dma((2 * NZ,)),
                dma((2 * S * S,)),
                dma((2 * S,)),
                dma((2 * S,)),
                dma((2 * S,)),
                dma((2 * NZ,)),
                dma((2 * NZ,)),
                dma((2,)),
                dma((2 * S,)),
                dma((2 * NZ,)),
                dma((2 * S,)),
            ],
            compiler_params=pltpu.CompilerParams(
                collective_id=0, has_side_effects=True, vmem_limit_bytes=60 * 2**20
            ),
        )(
            modality.reshape(1, T), gain_text.reshape(1, D), gain_image.reshape(1, D),
            tokens, cotangent, text_weight, image_weight,
        )
        return (*outs[:4], outs[4].reshape(D), outs[5].reshape(D))

    rows = P(("dp", "text", "image"), None)
    text_at, image_at = P(("dp", "image"), "text"), P(("dp", "text"), "image")
    return jax.shard_map(
        shards,
        mesh=mesh,
        in_specs=(rows, P(("dp", "text", "image")), P(), P(), text_at, image_at, rows),
        out_specs=(rows, rows, text_at, image_at, P(), P()),
        check_vma=False,
    )
```

```python
import functools

import jax
import jax.numpy as jnp
from jax import lax
from jax.experimental import pallas as pl
from jax.experimental.pallas import tpu as pltpu
from jax.sharding import PartitionSpec as P

MESH = pl.DeviceIdType.MESH
CAP = 72
EPSILON = 1e-05
F32 = jnp.float32
BF16 = jnp.bfloat16


def dot_nn(left, right):
    return jnp.dot(left, right, preferred_element_type=F32)


def dot_nt(left, right):
    return lax.dot_general(left, right, (((1,), (1,)), ((), ())), preferred_element_type=F32)


def dot_tn(left, right):
    return lax.dot_general(left, right, (((0,), (0,)), ((), ())), preferred_element_type=F32)


def ranks(modality, T):
    rows = lax.broadcasted_iota(jnp.int32, (T, T), 0)
    cols = lax.broadcasted_iota(jnp.int32, (T, T), 1)
    flag_row = jnp.where(modality == 0, 1.0, 0.0)
    wide = jnp.broadcast_to(flag_row, (T, T))
    flag_col = jnp.sum(jnp.where(rows == cols, wide, 0.0), axis=1, keepdims=True)
    rank_col = jnp.sum(jnp.where(cols < rows, wide, 0.0), axis=1, keepdims=True)
    tall = jnp.broadcast_to(flag_col, (T, T))
    rank_row = jnp.sum(jnp.where(rows < cols, tall, 0.0), axis=0, keepdims=True)
    return flag_row, flag_col, rank_row, rank_col


def layer(
    dims,
    mod_ref, gt_ref, gi_ref, tok_in, cot_in, wt_in, wi_in,
    qf_out, df_out, dw_out, dwx_out, gain_out,
    tok_ref, cot_ref, pick, flag, inv, work, gacc,
    xs, gs, xall, gall, w, qp, dp, qr, dm, dr, qf, df,
    dw_own, dw_peer, dw_sum, ring, dw_x, dw_xr, dw_end,
    g_core, g_b, g_z, g_c,
    local, send, x1, x2, g1, g2, wx, w1, w2, q1, q2, d0, d1, d2, e1, e2, e3, s1, s2, s3, s4,
):
    S, ZL, T, R, DS, ES = dims
    NZ = 2 * ZL
    H = NZ // 2
    CH = DS // ZL
    WR, WC = CH // 2, ES // 2
    WH = WR // 2
    D, E = DS * S, ES * S
    GR = DS // 128
    zl, text, image = lax.axis_index("dp"), lax.axis_index("text"), lax.axis_index("image")
    y, core = lax.div(text, 2), lax.rem(text, 2)
    x, zh = lax.div(image, 2), lax.rem(image, 2)
    z = zh * ZL + zl

    def cc(m):
        return x + (y - x) * m

    def bc(m):
        return y + (x - y) * m

    def odd(m):
        return lax.rem(cc(m), 2)

    def along_c(m, k):
        return (zl, lax.rem(text + 2 * k * m, 2 * S), lax.rem(image + 2 * k * (1 - m), 2 * S))

    def along_b(m, k):
        return (zl, lax.rem(text + 2 * k * (1 - m), 2 * S), lax.rem(image + 2 * k * m, 2 * S))

    def along_z(k):
        to = lax.rem(z + k, NZ)
        return (lax.rem(to, ZL), text, 2 * x + lax.div(to, ZL))

    def mate(m):
        return along_c(m, 1 + (S - 2) * lax.rem(cc(m) + core, 2))

    def twin(m):
        return along_c(m, 2)

    partner = (zl, text + 1 - 2 * core, image)

    def push(src, dst, send_sem, recv_sem, device):
        return pltpu.make_async_remote_copy(
            src_ref=src, dst_ref=dst, send_sem=send_sem, recv_sem=recv_sem,
            device_id=device, device_id_type=MESH,
        )

    def arrived(dst, recv_sem):
        push(dst, dst, send.at[21], recv_sem, partner).wait_recv()

    def sent(src, send_sem):
        push(src, src, send_sem, q1.at[0], partner).wait_send()

    barrier = pltpu.get_barrier_semaphore()

    @pl.loop(1, S)
    def _(k):
        pl.semaphore_signal(barrier, inc=1, device_id=along_c(0, k), device_id_type=MESH)
        pl.semaphore_signal(barrier, inc=1, device_id=along_b(0, k), device_id_type=MESH)

    @pl.loop(1, NZ)
    def _(k):
        pl.semaphore_signal(barrier, inc=1, device_id=along_z(k), device_id_type=MESH)

    pl.semaphore_signal(barrier, inc=1, device_id=partner, device_id_type=MESH)

    flag_row, flag_col, rank_row, _ = ranks(mod_ref[...], T)
    flag[...] = flag_col
    slot = lax.broadcasted_iota(jnp.int32, (R, T), 0).astype(F32)
    spot = lax.broadcasted_iota(jnp.int32, (R, T), 1).astype(F32)
    pick[:R] = jnp.where((rank_row == slot) & (flag_row > 0.5), 1.0, 0.0).astype(BF16)
    pick[R:] = jnp.where((spot - rank_row == slot) & (flag_row < 0.5), 1.0, 0.0).astype(BF16)

    def w_at(m, g, from_z, from_core, part=None):
        from_zh, from_zl = lax.div(from_z, ZL), lax.rem(from_z, ZL)
        half = from_core + (from_zh - from_core) * m
        row = 2 * from_zl + from_zh + (from_core - from_zh) * m
        if part is None:
            at = pl.ds(pl.multiple_of(row * WR, WR), WR)
        else:
            at = pl.ds(pl.multiple_of(row * WR + part * WH, WH), WH)
        return w.at[(m * 2 + g) * 2 + half, at, :]

    def group(m):
        return lax.div(cc(m), 2)

    loads = [
        pltpu.make_async_copy(wt_in, w_at(0, group(0), z, core), local.at[0]),
        pltpu.make_async_copy(wi_in, w_at(1, group(1), z, core), local.at[1]),
        pltpu.make_async_copy(cot_in, cot_ref, local.at[2]),
        pltpu.make_async_copy(tok_in, tok_ref, local.at[3]),
    ]
    for load in loads:
        load.start()

    def ring_w(t, m, g):
        lane = m * 2 + g
        if t < H:
            for way, step in ((0, 1), (1, NZ - 1)):
                block = w_at(m, g, lax.rem(z + (NZ - step) * (t - 1), NZ), core)
                push(block, block, send.at[18], w1.at[(way * H + t - 1) * 4 + lane], along_z(step)).start()
        else:
            for way, step in ((0, 1), (1, NZ - 1)):
                block = w_at(m, g, lax.rem(z + (NZ - step) * (t - 1), NZ), core, way)
                push(block, block, send.at[19], w1.at[(way * H + t - 1) * 4 + lane], along_z(step)).start()

    def ring_w_came(t, m, g):
        lane = m * 2 + g
        for way, step in ((0, 1), (1, NZ - 1)):
            origin = lax.rem(z + (NZ - step) * t, NZ)
            if t < H:
                block = w_at(m, g, origin, core)
                arrived(block, w1.at[(way * H + t - 1) * 4 + lane])
                push(block, block, send.at[1], w2.at[lane * NZ + origin], partner).start()
            else:
                arrived(w_at(m, g, origin, core, way), w1.at[(way * H + t - 1) * 4 + lane])
        if t == H:
            block = w_at(m, g, lax.rem(z + H, NZ), core)
            push(block, block, send.at[1], w2.at[lane * NZ + lax.rem(z + H, NZ)], partner).start()

    loads[0].wait()
    loads[1].wait()
    pl.semaphore_wait(barrier, 2 * (S - 1) + NZ)

    @pl.loop(0, 2)
    def _(m):
        mine = w_at(m, group(m), z, core)
        push(mine, mine, send.at[17], wx.at[m], twin(m)).start()
        ring_w(1, m, group(m))
        push(mine, mine, send.at[1], w2.at[(m * 2 + group(m)) * NZ + z], partner).start()

    loads[2].wait()

    @pl.loop(0, S)
    def _(b):
        part = cot_ref[:, pl.ds(pl.multiple_of(b * ES, ES), ES)]
        chosen = dot_nn(pick[...], part).astype(BF16)
        gs[b] = chosen[:R]
        gs[S + b] = chosen[R:]

    def token_rows(m, b, p):
        return (m * S + b) * 2 + p

    @pl.loop(0, 2)
    def _(m):
        mine = token_rows(m, bc(m), odd(m))
        gall[mine] = gs[m * S + bc(m)]

        @pl.loop(1, S)
        def _(j):
            to = lax.rem(bc(m) + j, S)
            push(gs.at[m * S + to], gall.at[mine], send.at[2], g1.at[m * S + j], along_b(m, j)).start()

        push(gall.at[mine], gall.at[mine], send.at[3], g2.at[m * S], mate(m)).start()

    loads[3].wait()
    squares = jnp.zeros((T, CH), F32)
    for i in range(S * ZL):
        part = tok_ref[:, i * CH:(i + 1) * CH].astype(F32)
        squares = squares + part * part
    inv[...] = lax.rsqrt(jnp.sum(squares, axis=1, keepdims=True) / D + EPSILON)

    @pl.loop(0, S * ZL)
    def _(i):
        c, zq = lax.div(i, ZL), lax.rem(i, ZL)
        at = pl.ds(pl.multiple_of(zq * (S * CH) + c * CH, CH), CH)
        to = pl.ds(pl.multiple_of(zq * CH, CH), CH)
        unit = tok_ref[:, at].astype(F32) * inv[...]
        gains = jnp.where(flag[...] > 0.5, gt_ref[:, at], gi_ref[:, at])
        normed = (unit * gains).astype(BF16)
        half, g = lax.rem(c, 2), lax.div(c, 2)
        chosen = dot_nn(pick[...], normed).astype(BF16)
        xs[half, g, :, to] = chosen[:R]
        xs[2 + half, g, :, to] = chosen[R:]

    def spread(m, kind):
        block = xall.at[token_rows(m, bc(m), odd(m) + kind - 2 * odd(m) * kind)]
        for way, step in ((0, 1), (1, S - 1)):
            push(block, block, send.at[5], x2.at[(m * 2 + kind) * 4 + way], along_b(m, step)).start()

    def spread_on(m, kind):
        p = odd(m) + kind - 2 * odd(m) * kind
        for way, step in ((0, 1), (1, S - 1)):
            block = xall.at[token_rows(m, lax.rem(bc(m) + S - step, S), p)]
            arrived(block, x2.at[(m * 2 + kind) * 4 + way])
            push(
                block.at[way], block.at[way], send.at[0], x2.at[(m * 2 + kind) * 4 + 2 + way],
                along_b(m, step),
            ).start()

    def spread_end(m, kind):
        p = odd(m) + kind - 2 * odd(m) * kind
        block = xall.at[token_rows(m, lax.rem(bc(m) + 2, S), p)]
        for way in range(2):
            arrived(block.at[way], x2.at[(m * 2 + kind) * 4 + 2 + way])

    def both(step, *rest):
        @pl.loop(0, 2)
        def _(m):
            step(m, *rest)

    @pl.loop(0, 2)
    def _(m):
        mine = token_rows(m, bc(m), odd(m))
        push(xs.at[m * 2 + 1 - odd(m)], xall.at[mine], send.at[4], x1.at[m], mate(m)).start()
        xall[mine] = xs[m * 2 + odd(m)]
        spread(m, 0)

    @pl.loop(0, 2)
    def _(m):
        other = 1 - group(m)
        block = w_at(m, other, z, core)
        arrived(block, wx.at[m])
        ring_w(1, m, other)
        push(block, block, send.at[1], w2.at[(m * 2 + other) * NZ + z], partner).start()

    def pass_on_grads(j):
        @pl.loop(0, 2)
        def _(m):
            block = gall.at[token_rows(m, lax.rem(bc(m) + S - j, S), odd(m))]
            arrived(block, g1.at[m * S + j])
            push(block, block, send.at[3], g2.at[m * S + j], mate(m)).start()

    def ring_w_on(t, kind):
        @pl.loop(0, 2)
        def _(m):
            g = group(m) + kind - 2 * group(m) * kind
            ring_w_came(t, m, g)
            if t < H:
                ring_w(t + 1, m, g)

    @pl.loop(0, 2)
    def _(m):
        arrived(xall.at[token_rows(m, bc(m), 1 - odd(m))], x1.at[m])
        spread(m, 1)

    pass_on_grads(1)
    ring_w_on(1, 0)
    pass_on_grads(3)
    pass_on_grads(2)
    ring_w_on(1, 1)
    both(spread_on, 0)
    if H > 1:
        ring_w_on(2, 0)
        ring_w_on(2, 1)
    both(spread_on, 1)
    for t in range(3, H + 1):
        ring_w_on(t, 0)
        ring_w_on(t, 1)
    both(spread_end, 0)
    both(spread_end, 1)

    @pl.loop(0, 2)
    def _(m):
        @pl.loop(0, S)
        def _(j):
            b = lax.rem(bc(m) + S - j, S)
            arrived(gall.at[token_rows(m, b, 1 - odd(m))], g2.at[m * S + j])

    def weight_grad(lane):
        m, g = lane // 2, lane % 2

        @pl.loop(0, ZL)
        def _(zq):
            at = pl.ds(pl.multiple_of(zq * CH, CH), CH)
            left = xall[pl.ds(m * 2 * S, 2 * S), g, :, at].reshape(2 * S * R, CH)
            for half in range(2):
                right = gall[pl.ds(m * 2 * S, 2 * S), :, half * WC:(half + 1) * WC]
                work[:, half * WC:(half + 1) * WC] = dot_tn(left, right.reshape(2 * S * R, WC))
            upper, lower = work[:WR, :WC], work[WR:, WC:]
            cross = (work[:WR, WC:], work[WR:, :WC])
            first, second = cross[m], cross[1 - m]
            low = core == 0
            dw_own[lane * NZ + zq] = jnp.where(low, upper, first).astype(BF16)
            dw_own[lane * NZ + ZL + zq] = jnp.where(low, second, lower).astype(BF16)
            dw_peer[lane * NZ + zq] = jnp.where(low, first, upper).astype(BF16)
            dw_peer[lane * NZ + ZL + zq] = jnp.where(low, lower, second).astype(BF16)
            for part in range(2):
                to = lane * NZ + part * ZL + zq
                push(dw_peer.at[to], dw_sum.at[to], send.at[10], e1.at[to], partner).start()

    def share(lane, to):
        return dw_own[lane * NZ + to].astype(F32) + dw_sum[lane * NZ + to].astype(F32)

    def ring_start(lane):
        to = lax.rem(z + H, NZ)
        at = lane * NZ + to
        arrived(dw_sum.at[at], e1.at[at])
        dw_own[at] = share(lane, to).astype(BF16)
        for way, step in ((0, 1), (1, NZ - 1)):
            half = pl.ds(way * WH, WH)
            push(
                dw_own.at[at, half], ring.at[(way * H) * 4 + lane, half], send.at[6],
                e2.at[(way * H) * 4 + lane], along_z(step),
            ).start()

    def ring_step(t, lane):
        for way, step in ((0, 1), (1, NZ - 1)):
            to = lax.rem(z + step * (H - t), NZ)
            at = (way * H + t - 1) * 4 + lane
            arrived(dw_sum.at[lane * NZ + to], e1.at[lane * NZ + to])
            own = share(lane, to)
            if t == 1:
                half, rest = pl.ds(way * WH, WH), pl.ds((1 - way) * WH, WH)
                arrived(ring.at[at, half], e2.at[at])
                total = ring[at, half].astype(F32) + own[way * WH:(way + 1) * WH]
                ring[at, half] = total.astype(BF16)
                ring[at, rest] = own[(1 - way) * WH:(2 - way) * WH].astype(BF16)
            else:
                arrived(ring.at[at], e2.at[at])
                ring[at] = (ring[at].astype(F32) + own).astype(BF16)
            push(ring.at[at], ring.at[at + 4], send.at[11], e2.at[at + 4], along_z(step)).start()

    def ring_end(lane):
        arrived(dw_sum.at[lane * NZ + z], e1.at[lane * NZ + z])
        total = share(lane, z)
        for way in range(2):
            at = (way * H + H - 1) * 4 + lane
            if H == 1:
                half, rest = pl.ds(way * WH, WH), pl.ds((1 - way) * WH, WH)
                arrived(ring.at[at, half], e2.at[at])
                ring[at, rest] = jnp.zeros((WH, WC), BF16)
            else:
                arrived(ring.at[at], e2.at[at])
            total = total + ring[at].astype(F32)
        return total

    def queries(m):
        @pl.loop(0, S // 2)
        def _(i):
            base = token_rows(m, 2 * i, 0)
            for half in range(2):
                total = jnp.zeros((4 * R, WC), F32)
                for g in range(2):
                    block = xall[pl.ds(base, 4), g].reshape(4 * R, DS)
                    total = total + dot_nn(block, w[(m * 2 + g) * 2 + half])
                qp[pl.ds(base, 4), :, half * WC:(half + 1) * WC] = total.astype(BF16).reshape(4, R, WC)
            for n in range(2):
                b = 2 * i + n
                push(
                    qp.at[token_rows(m, b, 1 - odd(m))], qr.at[m * S + b], send.at[7],
                    q1.at[m * S + b], mate(m),
                ).start()

    def input_grads(m, first, second):
        bases = [token_rows(m, lax.rem(bc(m) + step, S), 0) for step in (first, second)]

        def taken(ref, *at):
            return jnp.concatenate([ref[(pl.ds(base, 2), *at)] for base in bases], axis=0)

        for g in range(2):
            for part in range(2):
                at = slice(part * (DS // 2), (part + 1) * (DS // 2))
                total = dot_nt(
                    taken(gall, slice(None), slice(0, WC)).reshape(4 * R, WC), w[(m * 2 + g) * 2, at, :]
                ) + dot_nt(
                    taken(gall, slice(None), slice(WC, ES)).reshape(4 * R, WC), w[(m * 2 + g) * 2 + 1, at, :]
                )
                short = total.astype(BF16).reshape(4, R, DS // 2)
                dp[pl.ds(bases[0], 2), g, :, at] = short[:2]
                dp[pl.ds(bases[1], 2), g, :, at] = short[2:]
                rowed = taken(xall, g, slice(None), at).reshape(4 * R, DS // 2).astype(F32)
                gacc[m * 2 + g, :, at] += jnp.sum(total * rowed, axis=0, keepdims=True)

    def rows_to(m, step):
        return pl.ds(token_rows(m, lax.rem(bc(m) + step, S), 0), 2)

    def grads_near(m, way, g):
        push(
            dp.at[rows_to(m, (1, S - 1)[way]), g], dr.at[pl.ds((m * 2 + way) * 2, 2), g],
            send.at[8], d1.at[(m * 2 + way) * 2 + g], along_b(m, (1, S - 1)[way]),
        ).start()

    def input_grads_first(m):
        input_grads(m, 2, 1)
        for way in range(2):
            push(
                dp.at[rows_to(m, 2), way], dm.at[pl.ds((m * 2 + way) * 2, 2)],
                send.at[22], d0.at[m * 2 + way], along_b(m, (1, S - 1)[way]),
            ).start()
        grads_near(m, 0, 1)

    def input_grads_last(m):
        input_grads(m, S - 1, 0)
        grads_near(m, 1, 0)

    def input_grads_mid(m):
        for way in range(2):
            came = dm.at[pl.ds((m * 2 + way) * 2, 2)]
            arrived(came, d0.at[m * 2 + way])
            at = rows_to(m, (1, S - 1)[way])
            dp[at, way] = (dp[at, way].astype(F32) + came[...].astype(F32)).astype(BF16)
            grads_near(m, way, way)

    def gain_step(m, came, slots, going, place_at):
        total = came[m * slots]
        for i in range(1, slots):
            total = total + came[m * slots + i]
        going[place_at] = total

    def gains_core():
        @pl.loop(0, 2)
        def _(m):
            for g in range(2):
                for i in range(GR):
                    g_core[m * 2 + core, g * GR + i:g * GR + i + 1, :] = gacc[
                        m * 2 + g, :, i * 128:(i + 1) * 128
                    ]
            mine = g_core.at[m * 2 + core]
            push(mine, mine, send.at[9], s1.at[m], partner).start()

    def gains_b():
        @pl.loop(0, 2)
        def _(m):
            arrived(g_core.at[m * 2 + 1 - core], s1.at[m])
            gain_step(m, g_core, 2, g_b, m * S + bc(m))
            mine = g_b.at[m * S + bc(m)]

            @pl.loop(1, S)
            def _(j):
                push(mine, mine, send.at[12], s2.at[m * S + j], along_b(m, j)).start()

    def gains_z():
        @pl.loop(0, 2)
        def _(m):
            @pl.loop(1, S)
            def _(j):
                arrived(g_b.at[m * S + lax.rem(bc(m) + S - j, S)], s2.at[m * S + j])

            gain_step(m, g_b, S, g_z, m * NZ + z)
            mine = g_z.at[m * NZ + z]

            @pl.loop(1, NZ)
            def _(k):
                push(mine, mine, send.at[13], s3.at[m * NZ + k], along_z(k)).start()

    def gains_c():
        @pl.loop(0, 2)
        def _(m):
            @pl.loop(1, NZ)
            def _(k):
                arrived(g_z.at[m * NZ + lax.rem(z + NZ - k, NZ)], s3.at[m * NZ + k])

            gain_step(m, g_z, NZ, g_c, m * S + cc(m))
            mine = g_c.at[m * S + cc(m)]

            @pl.loop(1, S)
            def _(k):
                push(mine, mine, send.at[14], s4.at[m * S + k], along_c(m, k)).start()

    def query_sums(m):
        @pl.loop(1, S + 1)
        def _(j):
            b = lax.rem(bc(m) + j, S)
            mine = token_rows(m, b, odd(m))
            arrived(qr.at[m * S + b], q1.at[m * S + b])
            total = (qp[mine].astype(F32) + qr[m * S + b].astype(F32)).astype(BF16)

            @pl.when(j < S)
            def _():
                qp[mine] = total
                push(
                    qp.at[mine], qf.at[m * S + bc(m)], send.at[15], q2.at[m * S + j], along_b(m, j)
                ).start()

            @pl.when(j == S)
            def _():
                qf[m * S + bc(m)] = total

    def grad_sums(m):
        for way in range(2):
            for g in range(2):
                arrived(dr.at[pl.ds((m * 2 + way) * 2, 2), g], d1.at[(m * 2 + way) * 2 + g])

        def summed(p, g):
            total = dp[token_rows(m, bc(m), p), g].astype(F32)
            for way in range(2):
                total = total + dr[(m * 2 + way) * 2 + p, g].astype(F32)
            return total.astype(BF16)

        theirs = token_rows(m, bc(m), 1 - odd(m))
        for g in range(2):
            dp[theirs, g] = summed(1 - odd(m), g)
        push(dp.at[theirs], df.at[m * 2 + odd(m)], send.at[16], d2.at[m], mate(m)).start()
        for g in range(2):
            df[m * 2 + odd(m), g] = summed(odd(m), g)

    def steps(t, *lanes):
        if t < H:
            for lane in lanes:
                ring_step(t, lane)

    gacc[...] = jnp.zeros_like(gacc)
    weight_grad(0)

    @pl.loop(0, 4 * NZ)
    def _(i):
        lane, k = lax.div(i, NZ), lax.rem(i, NZ)
        m, g = lax.div(lane, 2), lax.rem(lane, 2)
        arrived(w_at(m, g, k, 1 - core), w2.at[lane * NZ + k])

    both(input_grads_first)
    ring_start(0)
    weight_grad(1)
    ring_start(1)
    steps(1, 0)
    both(input_grads_last)
    gains_core()
    input_grads_mid(0)
    weight_grad(2)
    ring_start(2)
    steps(1, 1)
    input_grads_mid(1)
    weight_grad(3)
    ring_start(3)
    steps(1, 2)
    steps(2, 0)
    queries(0)
    steps(1, 3)
    steps(2, 1)
    queries(1)
    gains_b()
    steps(2, 2, 3)
    query_sums(0)
    steps(3, 0)
    query_sums(1)
    steps(3, 1)
    gains_z()
    grad_sums(0)
    steps(3, 2)
    grad_sums(1)
    steps(3, 3)
    gains_c()

    @pl.loop(0, 2)
    def _(m):
        other = 1 - group(m)
        dw_x[m] = ring_end(m * 2 + other).astype(BF16)
        push(dw_x.at[m], dw_xr.at[m], send.at[20], e3.at[m], twin(m)).start()

    @pl.loop(0, 2)
    def _(m):
        @pl.loop(1, S)
        def _(j):
            arrived(qf.at[m * S + lax.rem(bc(m) + S - j, S)], q2.at[m * S + j])

    stores = [
        pltpu.make_async_copy(qf, qf_out, local.at[0]),
        pltpu.make_async_copy(df, df_out, local.at[1]),
        pltpu.make_async_copy(dw_end, dw_out, local.at[2]),
        pltpu.make_async_copy(dw_xr, dwx_out, local.at[3]),
        pltpu.make_async_copy(g_c, gain_out, local.at[4]),
    ]
    stores[0].start()

    @pl.loop(0, 2)
    def _(m):
        arrived(df.at[m * 2 + 1 - odd(m)], d2.at[m])

    stores[1].start()

    @pl.loop(0, 2)
    def _(m):
        dw_end[m] = ring_end(m * 2 + group(m))

    stores[2].start()

    @pl.loop(0, 2)
    def _(m):
        @pl.loop(1, S)
        def _(k):
            arrived(g_c.at[m * S + lax.rem(cc(m) + S - k, S)], s4.at[m * S + k])

    stores[4].start()

    @pl.loop(0, 2)
    def _(m):
        arrived(dw_xr.at[m], e3.at[m])

    stores[3].start()

    sent(w.at[pl.ds(0, 4)], send.at[1])
    sent(gs.at[pl.ds(0, 2 * (S - 1))], send.at[2])
    sent(gall.at[pl.ds(0, 2 * S)], send.at[3])
    sent(xs.at[pl.ds(0, 2)], send.at[4])
    sent(xall.at[pl.ds(0, 8)], send.at[5])
    sent(xall.at[pl.ds(0, 4)], send.at[0])
    sent(dw_own.at[pl.ds(0, 4)], send.at[6])
    sent(qp.at[pl.ds(0, 2 * S)], send.at[7])
    sent(dp.at[pl.ds(0, 8)], send.at[8])
    sent(dp.at[pl.ds(0, 4)], send.at[22])
    sent(g_core.at[pl.ds(0, 2)], send.at[9])
    sent(dw_peer, send.at[10])
    if H > 1:
        sent(ring.at[pl.ds(0, 8 * (H - 1))], send.at[11])
    sent(g_b.at[pl.ds(0, 2 * (S - 1))], send.at[12])
    sent(g_z.at[pl.ds(0, 2 * (NZ - 1))], send.at[13])
    sent(g_c.at[pl.ds(0, 2 * (S - 1))], send.at[14])
    sent(qp.at[pl.ds(0, 2 * (S - 1))], send.at[15])
    sent(dp.at[pl.ds(0, 2)], send.at[16])
    sent(dw_x, send.at[17])
    if H > 1:
        sent(ring.at[pl.ds(0, 8 * (H - 1))], send.at[18])
    sent(dw_own.at[pl.ds(0, 4)], send.at[19])
    sent(dw_x, send.at[20])
    for store in stores:
        store.wait()


def finish(
    dims,
    mod_ref, gt_ref, gi_ref, tok_ref, qf, df, dw_ref, dwx_ref, gain_ref,
    q_out, tg_out, dwt_out, dwi_out, ggt_out, ggi_out,
    grads,
):
    S, ZL, T, R, DS, ES = dims
    CH = DS // ZL
    GR = DS // 128
    D = DS * S
    _, flag, _, rank_col = ranks(mod_ref[...], T)
    slot = lax.broadcasted_iota(jnp.int32, (T, R), 1).astype(F32)
    spot = lax.broadcasted_iota(jnp.int32, (T, R), 0).astype(F32)
    text = jnp.where((rank_col == slot) & (flag > 0.5), 1.0, 0.0).astype(BF16)
    image = jnp.where((spot - rank_col == slot) & (flag < 0.5), 1.0, 0.0).astype(BF16)

    squares = jnp.zeros((T, CH), F32)
    products = jnp.zeros((T, CH), F32)
    for c in range(S):
        half, g = c % 2, c // 2
        normed_grad = dot_nn(text, df[half, g]) + dot_nn(image, df[2 + half, g])
        for zq in range(ZL):
            at = slice(zq * S * CH + c * CH, zq * S * CH + (c + 1) * CH)
            gains = jnp.where(flag > 0.5, gt_ref[:, at], gi_ref[:, at])
            part = normed_grad[:, zq * CH:(zq + 1) * CH] * gains
            token = tok_ref[:, at].astype(F32)
            grads[:, at] = part
            squares = squares + token * token
            products = products + part * token
    inv = lax.rsqrt(jnp.sum(squares, axis=1, keepdims=True) / D + EPSILON)
    along = jnp.sum(products, axis=1, keepdims=True) / D * inv * inv

    for i in range(S * ZL):
        at = slice(i * CH, (i + 1) * CH)
        tg_out[:, at] = (inv * (grads[:, at] - tok_ref[:, at].astype(F32) * along)).astype(BF16)

    for b in range(S):
        full = dot_nn(text, qf[b]) + dot_nn(image, qf[S + b])
        q_out[:, b * ES:(b + 1) * ES] = full.astype(BF16)

    dwt_out[...] = dw_ref[0] + dwx_ref[0].astype(F32)
    dwi_out[...] = dw_ref[1] + dwx_ref[1].astype(F32)

    for m, out, gain in ((0, ggt_out, gt_ref), (1, ggi_out, gi_ref)):
        for half in range(2):
            total = gain_ref[m * S + half]
            for k in range(half + 2, S, 2):
                total = total + gain_ref[m * S + k]
            for g in range(S // 2):
                for i in range(GR):
                    zq, off = (i * 128) // CH, (i * 128) % CH
                    first = zq * S * CH + (half + 2 * g) * CH + off
                    at = slice(first, first + 128)
                    out[:, at] = total[g * GR + i:g * GR + i + 1, :] / gain[:, at]


def solution(mesh):
    ZL, S = mesh.shape["dp"], mesh.shape["text"] // 2
    NZ = 2 * ZL
    H = NZ // 2

    def shards(tokens, modality, gain_text, gain_image, text_weight, image_weight, cotangent):
        T, D = tokens.shape
        E = cotangent.shape[1]
        R = -(-min(CAP, T) // 16) * 16
        DS, ES = D // S, E // S
        CH = DS // ZL
        WR, WC = CH // 2, ES // 2
        GR = DS // 128
        vmem = pl.BlockSpec(memory_space=pltpu.VMEM)
        dma = pltpu.SemaphoreType.DMA
        dims = (S, ZL, T, R, DS, ES)
        anywhere = pl.BlockSpec(memory_space=pl.ANY)
        modality, gain_text, gain_image = (
            modality.reshape(1, T), gain_text.reshape(1, D), gain_image.reshape(1, D)
        )
        parts = pl.pallas_call(
            functools.partial(layer, dims),
            out_shape=(
                jax.ShapeDtypeStruct((2 * S, R, ES), BF16),
                jax.ShapeDtypeStruct((4, 2, R, DS), BF16),
                jax.ShapeDtypeStruct((2, WR, WC), F32),
                jax.ShapeDtypeStruct((2, WR, WC), BF16),
                jax.ShapeDtypeStruct((2 * S, 2 * GR, 128), F32),
            ),
            in_specs=[vmem] * 3 + [anywhere] * 4,
            out_specs=(anywhere,) * 5,
            scratch_shapes=[
                pltpu.VMEM((T, D), BF16),
                pltpu.VMEM((T, E), BF16),
                pltpu.VMEM((2 * R, T), BF16),
                pltpu.VMEM((T, 1), F32),
                pltpu.VMEM((T, 1), F32),
                pltpu.VMEM((CH, ES), F32),
                pltpu.VMEM((4, 1, DS), F32),
                pltpu.VMEM((4, 2, R, DS), BF16),
                pltpu.VMEM((2 * S, R, ES), BF16),
                pltpu.VMEM((4 * S, 2, R, DS), BF16),
                pltpu.VMEM((4 * S, R, ES), BF16),
                pltpu.VMEM((8, DS, WC), BF16),
                pltpu.VMEM((4 * S, R, ES), BF16),
                pltpu.VMEM((4 * S, 2, R, DS), BF16),
                pltpu.VMEM((2 * S, R, ES), BF16),
                pltpu.VMEM((8, R, DS), BF16),
                pltpu.VMEM((8, 2, R, DS), BF16),
                pltpu.VMEM((2 * S, R, ES), BF16),
                pltpu.VMEM((4, 2, R, DS), BF16),
                pltpu.VMEM((4 * NZ, WR, WC), BF16),
                pltpu.VMEM((4 * NZ, WR, WC), BF16),
                pltpu.VMEM((4 * NZ, WR, WC), BF16),
                pltpu.VMEM((8 * H, WR, WC), BF16),
                pltpu.VMEM((2, WR, WC), BF16),
                pltpu.VMEM((2, WR, WC), BF16),
                pltpu.VMEM((2, WR, WC), F32),
                pltpu.VMEM((4, 2 * GR, 128), F32),
                pltpu.VMEM((2 * S, 2 * GR, 128), F32),
                pltpu.VMEM((2 * NZ, 2 * GR, 128), F32),
                pltpu.VMEM((2 * S, 2 * GR, 128), F32),
                dma((5,)),
                dma((23,)),
                dma((2,)),
                dma((16,)),
                dma((2 * S,)),
                dma((2 * S,)),
                dma((2,)),
                dma((8 * H,)),
                dma((4 * NZ,)),
                dma((2 * S,)),
                dma((2 * S,)),
                dma((4,)),
                dma((8,)),
                dma((2,)),
                dma((4 * NZ,)),
                dma((8 * H,)),
                dma((2,)),
                dma((2,)),
                dma((2 * S,)),
                dma((2 * NZ,)),
                dma((2 * S,)),
            ],
            compiler_params=pltpu.CompilerParams(
                collective_id=0, has_side_effects=True, vmem_limit_bytes=60 * 2**20
            ),
        )(modality, gain_text, gain_image, tokens, cotangent, text_weight, image_weight)
        outs = pl.pallas_call(
            functools.partial(finish, dims),
            out_shape=(
                jax.ShapeDtypeStruct((T, E), BF16),
                jax.ShapeDtypeStruct((T, D), BF16),
                jax.ShapeDtypeStruct((WR, WC), F32),
                jax.ShapeDtypeStruct((WR, WC), F32),
                jax.ShapeDtypeStruct((1, D), F32),
                jax.ShapeDtypeStruct((1, D), F32),
            ),
            in_specs=[vmem] * 9,
            out_specs=(vmem,) * 6,
            scratch_shapes=[pltpu.VMEM((T, D), F32)],
            compiler_params=pltpu.CompilerParams(vmem_limit_bytes=24 * 2**20),
        )(modality, gain_text, gain_image, tokens, *parts)
        return (*outs[:4], outs[4].reshape(D), outs[5].reshape(D))

    rows = P(("dp", "text", "image"), None)
    text_at, image_at = P(("dp", "image"), "text"), P(("dp", "text"), "image")
    return jax.shard_map(
        shards,
        mesh=mesh,
        in_specs=(rows, P(("dp", "text", "image")), P(), P(), text_at, image_at, rows),
        out_specs=(rows, rows, text_at, image_at, P(), P()),
        check_vma=False,
    )
```

```python
import functools

import jax
import jax.numpy as jnp
from jax import lax
from jax.experimental import pallas as pl
from jax.experimental.pallas import tpu as pltpu
from jax.sharding import PartitionSpec as P

MESH = pl.DeviceIdType.MESH
CAP = 72
EPSILON = 1e-05
F32 = jnp.float32
BF16 = jnp.bfloat16


def dot_nn(left, right):
    return jnp.dot(left, right, preferred_element_type=F32)


def dot_nt(left, right):
    return lax.dot_general(left, right, (((1,), (1,)), ((), ())), preferred_element_type=F32)


def dot_tn(left, right):
    return lax.dot_general(left, right, (((0,), (0,)), ((), ())), preferred_element_type=F32)


def ranks(modality, T):
    rows = lax.broadcasted_iota(jnp.int32, (T, T), 0)
    cols = lax.broadcasted_iota(jnp.int32, (T, T), 1)
    flag_row = jnp.where(modality == 0, 1.0, 0.0)
    wide = jnp.broadcast_to(flag_row, (T, T))
    flag_col = jnp.sum(jnp.where(rows == cols, wide, 0.0), axis=1, keepdims=True)
    rank_col = jnp.sum(jnp.where(cols < rows, wide, 0.0), axis=1, keepdims=True)
    tall = jnp.broadcast_to(flag_col, (T, T))
    rank_row = jnp.sum(jnp.where(rows < cols, tall, 0.0), axis=0, keepdims=True)
    return flag_row, flag_col, rank_row, rank_col


def layer(
    dims,
    mod_ref, gt_ref, gi_ref, tok_in, cot_in, wt_in, wi_in,
    q_out, tg_out, dwt_out, dwi_out, ggt_out, ggi_out,
    tok_ref, cot_ref, pick, place, flag, inv, work, grads, gacc,
    xs, gs, xall, gall, w, qp, dp, qr, dm, dr, qf, df,
    dw_own, dw_peer, dw_sum, ring, dw_x, dw_xr, dw_end,
    g_core, g_b, g_z, g_c, gain_ref,
    local, send, x1, x2, g1, g2, wx, w1, w2, q1, q2, d0, d1, d2, e1, e2, e3, s1, s2, s3, s4,
):
    S, ZL, T, R, DS, ES = dims
    NZ = 2 * ZL
    H = NZ // 2
    CH = DS // ZL
    WR, WC = CH // 2, ES // 2
    WH = WR // 2
    D, E = DS * S, ES * S
    GR = DS // 128
    zl, text, image = lax.axis_index("dp"), lax.axis_index("text"), lax.axis_index("image")
    y, core = lax.div(text, 2), lax.rem(text, 2)
    x, zh = lax.div(image, 2), lax.rem(image, 2)
    z = zh * ZL + zl

    def cc(m):
        return x + (y - x) * m

    def bc(m):
        return y + (x - y) * m

    def odd(m):
        return lax.rem(cc(m), 2)

    def along_c(m, k):
        return (zl, lax.rem(text + 2 * k * m, 2 * S), lax.rem(image + 2 * k * (1 - m), 2 * S))

    def along_b(m, k):
        return (zl, lax.rem(text + 2 * k * (1 - m), 2 * S), lax.rem(image + 2 * k * m, 2 * S))

    def along_z(k):
        to = lax.rem(z + k, NZ)
        return (lax.rem(to, ZL), text, 2 * x + lax.div(to, ZL))

    def mate(m):
        return along_c(m, 1 + (S - 2) * lax.rem(cc(m) + core, 2))

    def twin(m):
        return along_c(m, 2)

    partner = (zl, text + 1 - 2 * core, image)

    def push(src, dst, send_sem, recv_sem, device):
        return pltpu.make_async_remote_copy(
            src_ref=src, dst_ref=dst, send_sem=send_sem, recv_sem=recv_sem,
            device_id=device, device_id_type=MESH,
        )

    def arrived(dst, recv_sem):
        push(dst, dst, send.at[21], recv_sem, partner).wait_recv()

    def sent(src, send_sem):
        push(src, src, send_sem, q1.at[0], partner).wait_send()

    barrier = pltpu.get_barrier_semaphore()

    @pl.loop(1, S)
    def _(k):
        pl.semaphore_signal(barrier, inc=1, device_id=along_c(0, k), device_id_type=MESH)
        pl.semaphore_signal(barrier, inc=1, device_id=along_b(0, k), device_id_type=MESH)

    @pl.loop(1, NZ)
    def _(k):
        pl.semaphore_signal(barrier, inc=1, device_id=along_z(k), device_id_type=MESH)

    pl.semaphore_signal(barrier, inc=1, device_id=partner, device_id_type=MESH)

    flag_row, flag_col, rank_row, rank_col = ranks(mod_ref[...], T)
    flag[...] = flag_col
    slot = lax.broadcasted_iota(jnp.int32, (R, T), 0).astype(F32)
    spot = lax.broadcasted_iota(jnp.int32, (R, T), 1).astype(F32)
    pick[:R] = jnp.where((rank_row == slot) & (flag_row > 0.5), 1.0, 0.0).astype(BF16)
    pick[R:] = jnp.where((spot - rank_row == slot) & (flag_row < 0.5), 1.0, 0.0).astype(BF16)

    slot = lax.broadcasted_iota(jnp.int32, (T, R), 1).astype(F32)
    spot = lax.broadcasted_iota(jnp.int32, (T, R), 0).astype(F32)
    place[0] = jnp.where((rank_col == slot) & (flag_col > 0.5), 1.0, 0.0).astype(BF16)
    place[1] = jnp.where((spot - rank_col == slot) & (flag_col < 0.5), 1.0, 0.0).astype(BF16)

    def w_at(m, g, from_z, from_core, part=None):
        from_zh, from_zl = lax.div(from_z, ZL), lax.rem(from_z, ZL)
        half = from_core + (from_zh - from_core) * m
        row = 2 * from_zl + from_zh + (from_core - from_zh) * m
        if part is None:
            at = pl.ds(pl.multiple_of(row * WR, WR), WR)
        else:
            at = pl.ds(pl.multiple_of(row * WR + part * WH, WH), WH)
        return w.at[(m * 2 + g) * 2 + half, at, :]

    def group(m):
        return lax.div(cc(m), 2)

    loads = [
        pltpu.make_async_copy(wt_in, w_at(0, group(0), z, core), local.at[0]),
        pltpu.make_async_copy(wi_in, w_at(1, group(1), z, core), local.at[1]),
        pltpu.make_async_copy(cot_in, cot_ref, local.at[2]),
        pltpu.make_async_copy(tok_in, tok_ref, local.at[3]),
    ]
    for load in loads:
        load.start()

    def ring_w(t, m, g):
        lane = m * 2 + g
        if t < H:
            for way, step in ((0, 1), (1, NZ - 1)):
                block = w_at(m, g, lax.rem(z + (NZ - step) * (t - 1), NZ), core)
                push(block, block, send.at[18], w1.at[(way * H + t - 1) * 4 + lane], along_z(step)).start()
        else:
            for way, step in ((0, 1), (1, NZ - 1)):
                block = w_at(m, g, lax.rem(z + (NZ - step) * (t - 1), NZ), core, way)
                push(block, block, send.at[19], w1.at[(way * H + t - 1) * 4 + lane], along_z(step)).start()

    def ring_w_came(t, m, g):
        lane = m * 2 + g
        for way, step in ((0, 1), (1, NZ - 1)):
            origin = lax.rem(z + (NZ - step) * t, NZ)
            if t < H:
                block = w_at(m, g, origin, core)
                arrived(block, w1.at[(way * H + t - 1) * 4 + lane])
                push(block, block, send.at[1], w2.at[lane * NZ + origin], partner).start()
            else:
                arrived(w_at(m, g, origin, core, way), w1.at[(way * H + t - 1) * 4 + lane])
        if t == H:
            block = w_at(m, g, lax.rem(z + H, NZ), core)
            push(block, block, send.at[1], w2.at[lane * NZ + lax.rem(z + H, NZ)], partner).start()

    loads[0].wait()
    loads[1].wait()
    pl.semaphore_wait(barrier, 2 * (S - 1) + NZ)

    @pl.loop(0, 2)
    def _(m):
        mine = w_at(m, group(m), z, core)
        push(mine, mine, send.at[17], wx.at[m], twin(m)).start()
        ring_w(1, m, group(m))
        push(mine, mine, send.at[1], w2.at[(m * 2 + group(m)) * NZ + z], partner).start()

    loads[2].wait()

    @pl.loop(0, S)
    def _(b):
        part = cot_ref[:, pl.ds(pl.multiple_of(b * ES, ES), ES)]
        chosen = dot_nn(pick[...], part).astype(BF16)
        gs[b] = chosen[:R]
        gs[S + b] = chosen[R:]

    def token_rows(m, b, p):
        return (m * S + b) * 2 + p

    @pl.loop(0, 2)
    def _(m):
        mine = token_rows(m, bc(m), odd(m))
        gall[mine] = gs[m * S + bc(m)]

        @pl.loop(1, S)
        def _(j):
            to = lax.rem(bc(m) + j, S)
            push(gs.at[m * S + to], gall.at[mine], send.at[2], g1.at[m * S + j], along_b(m, j)).start()

        push(gall.at[mine], gall.at[mine], send.at[3], g2.at[m * S], mate(m)).start()

    loads[3].wait()
    squares = jnp.zeros((T, CH), F32)
    for i in range(S * ZL):
        part = tok_ref[:, i * CH:(i + 1) * CH].astype(F32)
        squares = squares + part * part
    inv[...] = lax.rsqrt(jnp.sum(squares, axis=1, keepdims=True) / D + EPSILON)

    scale = jnp.broadcast_to(inv[...], (T, CH))
    is_text = jnp.broadcast_to(flag[...], (T, CH)) > 0.5

    @pl.loop(0, S)
    def _(c):
        half, g = lax.rem(c, 2), lax.div(c, 2)
        for zq in range(ZL):
            at = pl.ds(pl.multiple_of(zq * (S * CH) + c * CH, CH), CH)
            gains = jnp.where(is_text, gt_ref[:, at], gi_ref[:, at])
            normed = (tok_ref[:, at].astype(F32) * scale * gains).astype(BF16)
            chosen = dot_nn(pick[...], normed).astype(BF16)
            xs[half, g, :, zq * CH:(zq + 1) * CH] = chosen[:R]
            xs[2 + half, g, :, zq * CH:(zq + 1) * CH] = chosen[R:]

    def spread(m, kind):
        block = xall.at[token_rows(m, bc(m), odd(m) + kind - 2 * odd(m) * kind)]
        for way, step in ((0, 1), (1, S - 1)):
            push(block, block, send.at[5], x2.at[(m * 2 + kind) * 4 + way], along_b(m, step)).start()

    def spread_on(m, kind):
        p = odd(m) + kind - 2 * odd(m) * kind
        for way, step in ((0, 1), (1, S - 1)):
            block = xall.at[token_rows(m, lax.rem(bc(m) + S - step, S), p)]
            arrived(block, x2.at[(m * 2 + kind) * 4 + way])
            push(
                block.at[way], block.at[way], send.at[0], x2.at[(m * 2 + kind) * 4 + 2 + way],
                along_b(m, step),
            ).start()

    def spread_end(m, kind):
        p = odd(m) + kind - 2 * odd(m) * kind
        block = xall.at[token_rows(m, lax.rem(bc(m) + 2, S), p)]
        for way in range(2):
            arrived(block.at[way], x2.at[(m * 2 + kind) * 4 + 2 + way])

    def both(step, *rest):
        @pl.loop(0, 2)
        def _(m):
            step(m, *rest)

    @pl.loop(0, 2)
    def _(m):
        mine = token_rows(m, bc(m), odd(m))
        push(xs.at[m * 2 + 1 - odd(m)], xall.at[mine], send.at[4], x1.at[m], mate(m)).start()
        xall[mine] = xs[m * 2 + odd(m)]
        spread(m, 0)

    @pl.loop(0, 2)
    def _(m):
        other = 1 - group(m)
        block = w_at(m, other, z, core)
        arrived(block, wx.at[m])
        ring_w(1, m, other)
        push(block, block, send.at[1], w2.at[(m * 2 + other) * NZ + z], partner).start()

    def pass_on_grads(j):
        @pl.loop(0, 2)
        def _(m):
            block = gall.at[token_rows(m, lax.rem(bc(m) + S - j, S), odd(m))]
            arrived(block, g1.at[m * S + j])
            push(block, block, send.at[3], g2.at[m * S + j], mate(m)).start()

    def ring_w_on(t, kind):
        @pl.loop(0, 2)
        def _(m):
            g = group(m) + kind - 2 * group(m) * kind
            ring_w_came(t, m, g)
            if t < H:
                ring_w(t + 1, m, g)

    ring_w_on(1, 0)
    pass_on_grads(1)
    pass_on_grads(3)
    pass_on_grads(2)
    ring_w_on(1, 1)

    @pl.loop(0, 2)
    def _(m):
        arrived(xall.at[token_rows(m, bc(m), 1 - odd(m))], x1.at[m])
        spread(m, 1)

    if H > 1:
        ring_w_on(2, 0)
    both(spread_on, 0)
    if H > 1:
        ring_w_on(2, 1)
    for t in range(3, H):
        ring_w_on(t, 0)
    both(spread_on, 1)
    for t in range(3, H):
        ring_w_on(t, 1)
    if H > 2:
        ring_w_on(H, 0)
        ring_w_on(H, 1)
    both(spread_end, 0)
    both(spread_end, 1)

    @pl.loop(0, 2)
    def _(m):
        @pl.loop(0, S)
        def _(j):
            b = lax.rem(bc(m) + S - j, S)
            arrived(gall.at[token_rows(m, b, 1 - odd(m))], g2.at[m * S + j])

    def lane_of(i):
        m = i % 2 if isinstance(i, int) else lax.rem(i, 2)
        far = 1 - (i // 2 if isinstance(i, int) else lax.div(i, 2))
        g = group(m) + (1 - 2 * group(m)) * far
        return m, g, m * 2 + g

    def weight_grad(m, first_offset, tiles):
        @pl.loop(0, tiles)
        def _(n):
            zq = lax.rem(zl + first_offset + n * (ZL - 2), ZL)
            at = pl.ds(pl.multiple_of(zq * CH, CH), CH)
            left = jnp.concatenate(
                [xall[pl.ds(m * 2 * S, 2 * S), g, :, at].reshape(2 * S * R, CH) for g in range(2)], axis=1
            )
            for half in range(2):
                right = gall[pl.ds(m * 2 * S, 2 * S), :, half * WC:(half + 1) * WC]
                work[:, half * WC:(half + 1) * WC] = dot_tn(left, right.reshape(2 * S * R, WC))
            low = core == 0
            for g in range(2):
                top, mid, end = g * CH, g * CH + WR, (g + 1) * CH
                base = (m * 2 + g) * NZ + zq
                upper, lower = work[top:mid, :WC], work[mid:end, WC:]
                cross = (work[top:mid, WC:], work[mid:end, :WC])
                first = jnp.where(m == 0, cross[0], cross[1])
                second = jnp.where(m == 0, cross[1], cross[0])
                dw_own[base] = jnp.where(low, upper, first).astype(BF16)
                dw_own[base + ZL] = jnp.where(low, second, lower).astype(BF16)
                dw_peer[base] = jnp.where(low, first, upper).astype(BF16)
                dw_peer[base + ZL] = jnp.where(low, lower, second).astype(BF16)
                for part in range(2):
                    to = base + part * ZL
                    push(dw_peer.at[to], dw_sum.at[to], send.at[10], e1.at[to], partner).start()

    def share(lane, to):
        return dw_own[lane * NZ + to].astype(F32) + dw_sum[lane * NZ + to].astype(F32)

    def ring_start(lane):
        to = lax.rem(z + H, NZ)
        at = lane * NZ + to
        arrived(dw_sum.at[at], e1.at[at])
        dw_own[at] = share(lane, to).astype(BF16)
        for way, step in ((0, 1), (1, NZ - 1)):
            half = pl.ds(way * WH, WH)
            push(
                dw_own.at[at, half], ring.at[(way * H) * 4 + lane, half], send.at[6],
                e2.at[(way * H) * 4 + lane], along_z(step),
            ).start()

    def ring_step(t, lane):
        for way, step in ((0, 1), (1, NZ - 1)):
            to = lax.rem(z + step * (H - t), NZ)
            at = (way * H + t - 1) * 4 + lane
            arrived(dw_sum.at[lane * NZ + to], e1.at[lane * NZ + to])
            own = share(lane, to)
            if t == 1:
                half, rest = pl.ds(way * WH, WH), pl.ds((1 - way) * WH, WH)
                arrived(ring.at[at, half], e2.at[at])
                total = ring[at, half].astype(F32) + own[way * WH:(way + 1) * WH]
                ring[at, half] = total.astype(BF16)
                ring[at, rest] = own[(1 - way) * WH:(2 - way) * WH].astype(BF16)
            else:
                arrived(ring.at[at], e2.at[at])
                ring[at] = (ring[at].astype(F32) + own).astype(BF16)
            push(ring.at[at], ring.at[at + 4], send.at[11], e2.at[at + 4], along_z(step)).start()

    def ring_end(lane):
        arrived(dw_sum.at[lane * NZ + z], e1.at[lane * NZ + z])
        total = share(lane, z)
        for way in range(2):
            at = (way * H + H - 1) * 4 + lane
            if H == 1:
                half, rest = pl.ds(way * WH, WH), pl.ds((1 - way) * WH, WH)
                arrived(ring.at[at, half], e2.at[at])
                ring[at, rest] = jnp.zeros((WH, WC), BF16)
            else:
                arrived(ring.at[at], e2.at[at])
            total = total + ring[at].astype(F32)
        return total

    def queries(m):
        @pl.loop(0, S // 2)
        def _(i):
            base = token_rows(m, 2 * i, 0)
            for half in range(2):
                total = jnp.zeros((4 * R, WC), F32)
                for g in range(2):
                    block = xall[pl.ds(base, 4), g].reshape(4 * R, DS)
                    total = total + dot_nn(block, w[(m * 2 + g) * 2 + half])
                qp[pl.ds(base, 4), :, half * WC:(half + 1) * WC] = total.astype(BF16).reshape(4, R, WC)
            for n in range(2):
                b = 2 * i + n
                push(
                    qp.at[token_rows(m, b, 1 - odd(m))], qr.at[m * S + b], send.at[7],
                    q1.at[m * S + b], mate(m),
                ).start()

    def input_grads(m, first, second):
        bases = [token_rows(m, lax.rem(bc(m) + step, S), 0) for step in (first, second)]

        def taken(ref, *at):
            return jnp.concatenate([ref[(pl.ds(base, 2), *at)] for base in bases], axis=0)

        for g in range(2):
            for part in range(2):
                at = slice(part * (DS // 2), (part + 1) * (DS // 2))
                total = dot_nt(
                    taken(gall, slice(None), slice(0, WC)).reshape(4 * R, WC), w[(m * 2 + g) * 2, at, :]
                ) + dot_nt(
                    taken(gall, slice(None), slice(WC, ES)).reshape(4 * R, WC), w[(m * 2 + g) * 2 + 1, at, :]
                )
                short = total.astype(BF16).reshape(4, R, DS // 2)
                dp[pl.ds(bases[0], 2), g, :, at] = short[:2]
                dp[pl.ds(bases[1], 2), g, :, at] = short[2:]
                rowed = taken(xall, g, slice(None), at).reshape(4 * R, DS // 2).astype(F32)
                gacc[m * 2 + g, :, at] += jnp.sum(total * rowed, axis=0, keepdims=True)

    def rows_to(m, step):
        return pl.ds(token_rows(m, lax.rem(bc(m) + step, S), 0), 2)

    def grads_near(m, way, g):
        push(
            dp.at[rows_to(m, (1, S - 1)[way]), g], dr.at[pl.ds((m * 2 + way) * 2, 2), g],
            send.at[8], d1.at[(m * 2 + way) * 2 + g], along_b(m, (1, S - 1)[way]),
        ).start()

    def input_grads_first(m):
        input_grads(m, 2, 1)
        for way in range(2):
            push(
                dp.at[rows_to(m, 2), way], dm.at[pl.ds((m * 2 + way) * 2, 2)],
                send.at[22], d0.at[m * 2 + way], along_b(m, (1, S - 1)[way]),
            ).start()
        grads_near(m, 0, 1)

    def input_grads_last(m):
        input_grads(m, S - 1, 0)
        grads_near(m, 1, 0)

    def input_grads_mid(m):
        for way in range(2):
            came = dm.at[pl.ds((m * 2 + way) * 2, 2)]
            arrived(came, d0.at[m * 2 + way])
            at = rows_to(m, (1, S - 1)[way])
            dp[at, way] = (dp[at, way].astype(F32) + came[...].astype(F32)).astype(BF16)
            grads_near(m, way, way)

    def gain_step(m, came, slots, going, place_at):
        total = came[m * slots]
        for i in range(1, slots):
            total = total + came[m * slots + i]
        going[place_at] = total

    def gains_core():
        @pl.loop(0, 2)
        def _(m):
            for g in range(2):
                for i in range(GR):
                    g_core[m * 2 + core, g * GR + i:g * GR + i + 1, :] = gacc[
                        m * 2 + g, :, i * 128:(i + 1) * 128
                    ]
            mine = g_core.at[m * 2 + core]
            push(mine, mine, send.at[9], s1.at[m], partner).start()

    def gains_b():
        @pl.loop(0, 2)
        def _(m):
            arrived(g_core.at[m * 2 + 1 - core], s1.at[m])
            gain_step(m, g_core, 2, g_b, m * S + bc(m))
            mine = g_b.at[m * S + bc(m)]

            @pl.loop(1, S)
            def _(j):
                push(mine, mine, send.at[12], s2.at[m * S + j], along_b(m, j)).start()

    def gains_z():
        @pl.loop(0, 2)
        def _(m):
            @pl.loop(1, S)
            def _(j):
                arrived(g_b.at[m * S + lax.rem(bc(m) + S - j, S)], s2.at[m * S + j])

            gain_step(m, g_b, S, g_z, m * NZ + z)
            mine = g_z.at[m * NZ + z]

            @pl.loop(1, NZ)
            def _(k):
                push(mine, mine, send.at[13], s3.at[m * NZ + k], along_z(k)).start()

    def gains_c():
        @pl.loop(0, 2)
        def _(m):
            @pl.loop(1, NZ)
            def _(k):
                arrived(g_z.at[m * NZ + lax.rem(z + NZ - k, NZ)], s3.at[m * NZ + k])

            gain_step(m, g_z, NZ, g_c, m * S + cc(m))
            mine = g_c.at[m * S + cc(m)]

            @pl.loop(1, S)
            def _(k):
                push(mine, mine, send.at[14], s4.at[m * S + k], along_c(m, k)).start()

    def query_sums(m):
        @pl.loop(1, S + 1)
        def _(j):
            b = lax.rem(bc(m) + j, S)
            mine = token_rows(m, b, odd(m))
            arrived(qr.at[m * S + b], q1.at[m * S + b])
            total = (qp[mine].astype(F32) + qr[m * S + b].astype(F32)).astype(BF16)

            @pl.when(j < S)
            def _():
                qp[mine] = total
                push(
                    qp.at[mine], qf.at[m * S + bc(m)], send.at[15], q2.at[m * S + j], along_b(m, j)
                ).start()

            @pl.when(j == S)
            def _():
                qf[m * S + bc(m)] = total

    def grad_sums(m):
        for way in range(2):
            for g in range(2):
                arrived(dr.at[pl.ds((m * 2 + way) * 2, 2), g], d1.at[(m * 2 + way) * 2 + g])

        def summed(p, g):
            total = dp[token_rows(m, bc(m), p), g].astype(F32)
            for way in range(2):
                total = total + dr[(m * 2 + way) * 2 + p, g].astype(F32)
            return total.astype(BF16)

        theirs = token_rows(m, bc(m), 1 - odd(m))
        for g in range(2):
            dp[theirs, g] = summed(1 - odd(m), g)
        push(dp.at[theirs], df.at[m * 2 + odd(m)], send.at[16], d2.at[m], mate(m)).start()
        for g in range(2):
            df[m * 2 + odd(m), g] = summed(odd(m), g)

    def steps(t, *lanes):
        if t < H:
            for lane in lanes:
                ring_step(t, lane_of(lane)[2])

    gacc[...] = jnp.zeros_like(gacc)
    both(weight_grad, 0, 1)

    @pl.loop(0, 4 * NZ)
    def _(i):
        lane, k = lax.div(i, NZ), lax.rem(i, NZ)
        m, g = lax.div(lane, 2), lax.rem(lane, 2)
        arrived(w_at(m, g, k, 1 - core), w2.at[lane * NZ + k])

    input_grads_first(0)
    ring_start(lane_of(0)[2])
    ring_start(lane_of(1)[2])
    input_grads_first(1)
    ring_start(lane_of(2)[2])
    ring_start(lane_of(3)[2])
    @pl.loop(0, 2)
    def _(m):
        weight_grad(m, 1, 2)
        ring_step(1, lane_of(m)[2])
        ring_step(1, lane_of(m + 2)[2])

    input_grads_last(0)
    input_grads_last(1)
    gains_core()
    input_grads_mid(0)
    input_grads_mid(1)

    both(weight_grad, 2, 1)

    gains_b()
    steps(2, 0, 1)
    queries(0)
    steps(2, 2, 3)
    queries(1)
    steps(3, 0, 1)
    gains_z()
    both(grad_sums)
    steps(3, 2, 3)
    query_sums(0)
    gains_c()
    query_sums(1)

    @pl.loop(0, 2)
    def _(m):
        other = 1 - group(m)
        dw_x[m] = ring_end(m * 2 + other).astype(BF16)
        push(dw_x.at[m], dw_xr.at[m], send.at[20], e3.at[m], twin(m)).start()

    @pl.loop(0, 2)
    def _(m):
        @pl.loop(1, S)
        def _(j):
            arrived(qf.at[m * S + lax.rem(bc(m) + S - j, S)], q2.at[m * S + j])

    @pl.loop(0, S)
    def _(b):
        full = dot_nn(place[0], qf[b]) + dot_nn(place[1], qf[S + b])
        cot_ref[:, pl.ds(pl.multiple_of(b * ES, ES), ES)] = full.astype(BF16)

    stores = [
        pltpu.make_async_copy(cot_ref, q_out, local.at[0]),
        pltpu.make_async_copy(tok_ref, tg_out, local.at[1]),
        pltpu.make_async_copy(dw_end.at[0], dwt_out, local.at[2]),
        pltpu.make_async_copy(dw_end.at[1], dwi_out, local.at[3]),
        pltpu.make_async_copy(gain_ref.at[0], ggt_out, local.at[4]),
        pltpu.make_async_copy(gain_ref.at[1], ggi_out, local.at[5]),
    ]
    stores[0].start()

    @pl.loop(0, 2)
    def _(m):
        arrived(df.at[m * 2 + 1 - odd(m)], d2.at[m])

    products = jnp.zeros((T, CH), F32)
    for c in range(S):
        half, g = c % 2, c // 2
        normed_grad = dot_nn(place[0], df[half, g]) + dot_nn(place[1], df[2 + half, g])
        for zq in range(ZL):
            at = slice(zq * S * CH + c * CH, zq * S * CH + (c + 1) * CH)
            gains = jnp.where(flag[...] > 0.5, gt_ref[:, at], gi_ref[:, at])
            part = normed_grad[:, zq * CH:(zq + 1) * CH] * gains
            grads[:, at] = part
            products = products + part * tok_ref[:, at].astype(F32)
    scale = inv[...]
    along = jnp.sum(products, axis=1, keepdims=True) / D * scale * scale
    for i in range(S * ZL):
        at = slice(i * CH, (i + 1) * CH)
        tok_ref[:, at] = (scale * (grads[:, at] - tok_ref[:, at].astype(F32) * along)).astype(BF16)

    stores[1].start()

    @pl.loop(0, 2)
    def _(m):
        @pl.loop(1, S)
        def _(k):
            arrived(g_c.at[m * S + lax.rem(cc(m) + S - k, S)], s4.at[m * S + k])

    for m, gain in ((0, gt_ref), (1, gi_ref)):
        for half in range(2):
            total = g_c[m * S + half]
            for k in range(half + 2, S, 2):
                total = total + g_c[m * S + k]
            for g in range(S // 2):
                for i in range(GR):
                    zq, off = (i * 128) // CH, (i * 128) % CH
                    first = zq * S * CH + (half + 2 * g) * CH + off
                    at = slice(first, first + 128)
                    gain_ref[m, :, at] = total[g * GR + i:g * GR + i + 1, :] / gain[:, at]

    stores[4].start()
    stores[5].start()

    @pl.loop(0, 2)
    def _(m):
        own = ring_end(m * 2 + group(m))
        arrived(dw_xr.at[m], e3.at[m])
        dw_end[m] = own + dw_xr[m].astype(F32)

    stores[2].start()
    stores[3].start()

    sent(w.at[pl.ds(0, 4)], send.at[1])
    sent(gs.at[pl.ds(0, 2 * (S - 1))], send.at[2])
    sent(gall.at[pl.ds(0, 2 * S)], send.at[3])
    sent(xs.at[pl.ds(0, 2)], send.at[4])
    sent(xall.at[pl.ds(0, 8)], send.at[5])
    sent(xall.at[pl.ds(0, 4)], send.at[0])
    sent(dw_own.at[pl.ds(0, 4)], send.at[6])
    sent(qp.at[pl.ds(0, 2 * S)], send.at[7])
    sent(dp.at[pl.ds(0, 8)], send.at[8])
    sent(dp.at[pl.ds(0, 4)], send.at[22])
    sent(g_core.at[pl.ds(0, 2)], send.at[9])
    sent(dw_peer, send.at[10])
    if H > 1:
        sent(ring.at[pl.ds(0, 8 * (H - 1))], send.at[11])
    sent(g_b.at[pl.ds(0, 2 * (S - 1))], send.at[12])
    sent(g_z.at[pl.ds(0, 2 * (NZ - 1))], send.at[13])
    sent(g_c.at[pl.ds(0, 2 * (S - 1))], send.at[14])
    sent(qp.at[pl.ds(0, 2 * (S - 1))], send.at[15])
    sent(dp.at[pl.ds(0, 2)], send.at[16])
    sent(dw_x, send.at[17])
    if H > 1:
        sent(ring.at[pl.ds(0, 8 * (H - 1))], send.at[18])
    sent(dw_own.at[pl.ds(0, 4)], send.at[19])
    sent(dw_x, send.at[20])
    for store in stores:
        store.wait()


def hand_on(*refs):
    came, gone = refs[-2:]
    count = (len(refs) - 2) // 3
    sources, targets, held = refs[:count], refs[count:2 * count], refs[2 * count:3 * count]
    loads = [pltpu.make_async_copy(sources[i], held[i], came.at[i]) for i in range(count)]
    stores = [pltpu.make_async_copy(held[i], targets[i], gone.at[i]) for i in range(count)]
    for load in loads:
        load.start()
    for load, store in zip(loads, stores):
        load.wait()
        store.start()
    for store in stores:
        store.wait()


def solution(mesh):
    ZL, S = mesh.shape["dp"], mesh.shape["text"] // 2
    NZ = 2 * ZL
    H = NZ // 2

    def shards(tokens, modality, gain_text, gain_image, text_weight, image_weight, cotangent):
        T, D = tokens.shape
        E = cotangent.shape[1]
        R = -(-min(CAP, T) // 16) * 16
        DS, ES = D // S, E // S
        CH = DS // ZL
        WR, WC = CH // 2, ES // 2
        GR = DS // 128
        vmem = pl.BlockSpec(memory_space=pltpu.VMEM)
        dma = pltpu.SemaphoreType.DMA
        dims = (S, ZL, T, R, DS, ES)
        anywhere = pl.BlockSpec(memory_space=pl.ANY)
        modality, gain_text, gain_image = (
            modality.reshape(1, T), gain_text.reshape(1, D), gain_image.reshape(1, D)
        )
        shapes = (
            jax.ShapeDtypeStruct((T, E), BF16),
            jax.ShapeDtypeStruct((T, D), BF16),
            jax.ShapeDtypeStruct((WR, WC), F32),
            jax.ShapeDtypeStruct((WR, WC), F32),
            jax.ShapeDtypeStruct((1, D), F32),
            jax.ShapeDtypeStruct((1, D), F32),
        )
        parts = pl.pallas_call(
            functools.partial(layer, dims),
            out_shape=shapes,
            in_specs=[vmem] * 3 + [anywhere] * 4,
            out_specs=(anywhere,) * 6,
            scratch_shapes=[
                pltpu.VMEM((T, D), BF16),
                pltpu.VMEM((T, E), BF16),
                pltpu.VMEM((2 * R, T), BF16),
                pltpu.VMEM((2, T, R), BF16),
                pltpu.VMEM((T, 1), F32),
                pltpu.VMEM((T, 1), F32),
                pltpu.VMEM((2 * CH, ES), F32),
                pltpu.VMEM((T, D), F32),
                pltpu.VMEM((4, 1, DS), F32),
                pltpu.VMEM((4, 2, R, DS), BF16),
                pltpu.VMEM((2 * S, R, ES), BF16),
                pltpu.VMEM((4 * S, 2, R, DS), BF16),
                pltpu.VMEM((4 * S, R, ES), BF16),
                pltpu.VMEM((8, DS, WC), BF16),
                pltpu.VMEM((4 * S, R, ES), BF16),
                pltpu.VMEM((4 * S, 2, R, DS), BF16),
                pltpu.VMEM((2 * S, R, ES), BF16),
                pltpu.VMEM((8, R, DS), BF16),
                pltpu.VMEM((8, 2, R, DS), BF16),
                pltpu.VMEM((2 * S, R, ES), BF16),
                pltpu.VMEM((4, 2, R, DS), BF16),
                pltpu.VMEM((4 * NZ, WR, WC), BF16),
                pltpu.VMEM((4 * NZ, WR, WC), BF16),
                pltpu.VMEM((4 * NZ, WR, WC), BF16),
                pltpu.VMEM((8 * H, WR, WC), BF16),
                pltpu.VMEM((2, WR, WC), BF16),
                pltpu.VMEM((2, WR, WC), BF16),
                pltpu.VMEM((2, WR, WC), F32),
                pltpu.VMEM((4, 2 * GR, 128), F32),
                pltpu.VMEM((2 * S, 2 * GR, 128), F32),
                pltpu.VMEM((2 * NZ, 2 * GR, 128), F32),
                pltpu.VMEM((2 * S, 2 * GR, 128), F32),
                pltpu.VMEM((2, 1, D), F32),
                dma((6,)),
                dma((23,)),
                dma((2,)),
                dma((16,)),
                dma((2 * S,)),
                dma((2 * S,)),
                dma((2,)),
                dma((8 * H,)),
                dma((4 * NZ,)),
                dma((2 * S,)),
                dma((2 * S,)),
                dma((4,)),
                dma((8,)),
                dma((2,)),
                dma((4 * NZ,)),
                dma((8 * H,)),
                dma((2,)),
                dma((2,)),
                dma((2 * S,)),
                dma((2 * NZ,)),
                dma((2 * S,)),
            ],
            compiler_params=pltpu.CompilerParams(
                collective_id=0, has_side_effects=True, vmem_limit_bytes=60 * 2**20
            ),
        )(modality, gain_text, gain_image, tokens, cotangent, text_weight, image_weight)
        outs = pl.pallas_call(
            hand_on,
            out_shape=shapes,
            in_specs=[anywhere] * 6,
            out_specs=(anywhere,) * 6,
            scratch_shapes=[pltpu.VMEM(a.shape, a.dtype) for a in shapes] + [dma((6,)), dma((6,))],
            compiler_params=pltpu.CompilerParams(vmem_limit_bytes=60 * 2**20),
        )(*parts)
        return (*outs[:4], outs[4].reshape(D), outs[5].reshape(D))

    rows = P(("dp", "text", "image"), None)
    text_at, image_at = P(("dp", "image"), "text"), P(("dp", "text"), "image")
    return jax.shard_map(
        shards,
        mesh=mesh,
        in_specs=(rows, P(("dp", "text", "image")), P(), P(), text_at, image_at, rows),
        out_specs=(rows, rows, text_at, image_at, P(), P()),
        check_vma=False,
    )
```

```python
import functools

import jax
import jax.numpy as jnp
from jax import lax
from jax.experimental import pallas as pl
from jax.experimental.pallas import tpu as pltpu
from jax.sharding import PartitionSpec as P

MESH = pl.DeviceIdType.MESH
CAP = 72
EPSILON = 1e-05
F32 = jnp.float32
BF16 = jnp.bfloat16


def dot_nn(left, right):
    return jnp.dot(left, right, preferred_element_type=F32)


def dot_nt(left, right):
    return lax.dot_general(left, right, (((1,), (1,)), ((), ())), preferred_element_type=F32)


def dot_tn(left, right):
    return lax.dot_general(left, right, (((0,), (0,)), ((), ())), preferred_element_type=F32)


def ranks(modality, T):
    rows = lax.broadcasted_iota(jnp.int32, (T, T), 0)
    cols = lax.broadcasted_iota(jnp.int32, (T, T), 1)
    flag_row = jnp.where(modality == 0, 1.0, 0.0)
    wide = jnp.broadcast_to(flag_row, (T, T))
    flag_col = jnp.sum(jnp.where(rows == cols, wide, 0.0), axis=1, keepdims=True)
    rank_col = jnp.sum(jnp.where(cols < rows, wide, 0.0), axis=1, keepdims=True)
    tall = jnp.broadcast_to(flag_col, (T, T))
    rank_row = jnp.sum(jnp.where(rows < cols, tall, 0.0), axis=0, keepdims=True)
    return flag_row, flag_col, rank_row, rank_col


def layer(
    dims,
    mod_ref, gt_ref, gi_ref, tok_in, cot_in, wt_in, wi_in,
    q_out, tg_out, dwt_out, dwi_out, ggt_out, ggi_out,
    tok_ref, cot_ref, pick, place, flag, inv, work, grads, gacc,
    xs, gs, xall, gall, w, qp, dp, qr, dm, dr, qf, df,
    dw_own, dw_peer, dw_sum, ring, dw_x, dw_xr, dw_end,
    g_core, g_b, g_z, g_c, gain_ref,
    local, send, x1, x2, g1, g2, wx, w1, w2, q1, q2, d0, d1, d2, e1, e2, e3, s1, s2, s3, s4,
):
    S, ZL, T, R, DS, ES = dims
    NZ = 2 * ZL
    H = NZ // 2
    CH = DS // ZL
    WR, WC = CH // 2, ES // 2
    WH = WR // 2
    D, E = DS * S, ES * S
    GR = DS // 128
    zl, text, image = lax.axis_index("dp"), lax.axis_index("text"), lax.axis_index("image")
    y, core = lax.div(text, 2), lax.rem(text, 2)
    x, zh = lax.div(image, 2), lax.rem(image, 2)
    z = zh * ZL + zl

    def cc(m):
        return x + (y - x) * m

    def bc(m):
        return y + (x - y) * m

    def odd(m):
        return lax.rem(cc(m), 2)

    def along_c(m, k):
        return (zl, lax.rem(text + 2 * k * m, 2 * S), lax.rem(image + 2 * k * (1 - m), 2 * S))

    def along_b(m, k):
        return (zl, lax.rem(text + 2 * k * (1 - m), 2 * S), lax.rem(image + 2 * k * m, 2 * S))

    def along_z(k):
        to = lax.rem(z + k, NZ)
        return (lax.rem(to, ZL), text, 2 * x + lax.div(to, ZL))

    def mate(m):
        return along_c(m, 1 + (S - 2) * lax.rem(cc(m) + core, 2))

    def twin(m):
        return along_c(m, 2)

    partner = (zl, text + 1 - 2 * core, image)

    def push(src, dst, send_sem, recv_sem, device):
        return pltpu.make_async_remote_copy(
            src_ref=src, dst_ref=dst, send_sem=send_sem, recv_sem=recv_sem,
            device_id=device, device_id_type=MESH,
        )

    def arrived(dst, recv_sem):
        push(dst, dst, send.at[21], recv_sem, partner).wait_recv()

    def sent(src, send_sem):
        push(src, src, send_sem, q1.at[0], partner).wait_send()

    barrier = pltpu.get_barrier_semaphore()

    @pl.loop(1, S)
    def _(k):
        pl.semaphore_signal(barrier, inc=1, device_id=along_c(0, k), device_id_type=MESH)
        pl.semaphore_signal(barrier, inc=1, device_id=along_b(0, k), device_id_type=MESH)

    @pl.loop(1, NZ)
    def _(k):
        pl.semaphore_signal(barrier, inc=1, device_id=along_z(k), device_id_type=MESH)

    pl.semaphore_signal(barrier, inc=1, device_id=partner, device_id_type=MESH)

    def w_at(m, g, from_z, from_core, part=None):
        from_zh, from_zl = lax.div(from_z, ZL), lax.rem(from_z, ZL)
        half = from_core + (from_zh - from_core) * m
        row = 2 * from_zl + from_zh + (from_core - from_zh) * m
        if part is None:
            at = pl.ds(pl.multiple_of(row * WR, WR), WR)
        else:
            at = pl.ds(pl.multiple_of(row * WR + part * WH, WH), WH)
        return w.at[(m * 2 + g) * 2 + half, at, :]

    def group(m):
        return lax.div(cc(m), 2)

    loads = [
        pltpu.make_async_copy(wt_in, w_at(0, group(0), z, core), local.at[0]),
        pltpu.make_async_copy(wi_in, w_at(1, group(1), z, core), local.at[1]),
        pltpu.make_async_copy(cot_in, cot_ref, local.at[2]),
        pltpu.make_async_copy(tok_in, tok_ref, local.at[3]),
    ]
    for load in loads:
        load.start()

    def ring_w(t, m, g):
        lane = m * 2 + g
        if t < H:
            for way, step in ((0, 1), (1, NZ - 1)):
                block = w_at(m, g, lax.rem(z + (NZ - step) * (t - 1), NZ), core)
                push(block, block, send.at[18], w1.at[(way * H + t - 1) * 4 + lane], along_z(step)).start()
        else:
            for way, step in ((0, 1), (1, NZ - 1)):
                block = w_at(m, g, lax.rem(z + (NZ - step) * (t - 1), NZ), core, way)
                push(block, block, send.at[19], w1.at[(way * H + t - 1) * 4 + lane], along_z(step)).start()

    def ring_w_came(t, m, g):
        lane = m * 2 + g
        for way, step in ((0, 1), (1, NZ - 1)):
            origin = lax.rem(z + (NZ - step) * t, NZ)
            if t < H:
                block = w_at(m, g, origin, core)
                arrived(block, w1.at[(way * H + t - 1) * 4 + lane])
                push(block, block, send.at[1], w2.at[lane * NZ + origin], partner).start()
            else:
                arrived(w_at(m, g, origin, core, way), w1.at[(way * H + t - 1) * 4 + lane])
        if t == H:
            block = w_at(m, g, lax.rem(z + H, NZ), core)
            push(block, block, send.at[1], w2.at[lane * NZ + lax.rem(z + H, NZ)], partner).start()

    pl.semaphore_wait(barrier, 2 * (S - 1) + NZ)
    for m, mine in ((0, wt_in), (1, wi_in)):
        lane = m * 2 + group(m)
        place_at = w_at(m, group(m), z, core)
        for way, step in ((0, 1), (1, NZ - 1)):
            push(mine, place_at, send.at[18], w1.at[way * H * 4 + lane], along_z(step)).start()
        push(mine, place_at, send.at[17], wx.at[m], twin(m)).start()
        push(mine, place_at, send.at[1], w2.at[lane * NZ + z], partner).start()

    flag_row, flag_col, rank_row, rank_col = ranks(mod_ref[...], T)
    flag[...] = flag_col
    slot = lax.broadcasted_iota(jnp.int32, (R, T), 0).astype(F32)
    spot = lax.broadcasted_iota(jnp.int32, (R, T), 1).astype(F32)
    pick[:R] = jnp.where((rank_row == slot) & (flag_row > 0.5), 1.0, 0.0).astype(BF16)
    pick[R:] = jnp.where((spot - rank_row == slot) & (flag_row < 0.5), 1.0, 0.0).astype(BF16)

    slot = lax.broadcasted_iota(jnp.int32, (T, R), 1).astype(F32)
    spot = lax.broadcasted_iota(jnp.int32, (T, R), 0).astype(F32)
    place[0] = jnp.where((rank_col == slot) & (flag_col > 0.5), 1.0, 0.0).astype(BF16)
    place[1] = jnp.where((spot - rank_col == slot) & (flag_col < 0.5), 1.0, 0.0).astype(BF16)

    loads[2].wait()

    @pl.loop(0, S)
    def _(b):
        part = cot_ref[:, pl.ds(pl.multiple_of(b * ES, ES), ES)]
        chosen = dot_nn(pick[...], part).astype(BF16)
        gs[b] = chosen[:R]
        gs[S + b] = chosen[R:]

    def token_rows(m, b, p):
        return (m * S + b) * 2 + p

    @pl.loop(0, 2)
    def _(m):
        mine = token_rows(m, bc(m), odd(m))
        gall[mine] = gs[m * S + bc(m)]

        @pl.loop(1, S)
        def _(j):
            to = lax.rem(bc(m) + j, S)
            push(gs.at[m * S + to], gall.at[mine], send.at[2], g1.at[m * S + j], along_b(m, j)).start()

        push(gall.at[mine], gall.at[mine], send.at[3], g2.at[m * S], mate(m)).start()

    loads[3].wait()
    squares = jnp.zeros((T, CH), F32)
    for i in range(S * ZL):
        part = tok_ref[:, i * CH:(i + 1) * CH].astype(F32)
        squares = squares + part * part
    inv[...] = lax.rsqrt(jnp.sum(squares, axis=1, keepdims=True) / D + EPSILON)

    scale = jnp.broadcast_to(inv[...], (T, CH))
    is_text = jnp.broadcast_to(flag[...], (T, CH)) > 0.5

    @pl.loop(0, S)
    def _(c):
        half, g = lax.rem(c, 2), lax.div(c, 2)
        for zq in range(ZL):
            at = pl.ds(pl.multiple_of(zq * (S * CH) + c * CH, CH), CH)
            gains = jnp.where(is_text, gt_ref[:, at], gi_ref[:, at])
            normed = (tok_ref[:, at].astype(F32) * scale * gains).astype(BF16)
            chosen = dot_nn(pick[...], normed).astype(BF16)
            xs[half, g, :, zq * CH:(zq + 1) * CH] = chosen[:R]
            xs[2 + half, g, :, zq * CH:(zq + 1) * CH] = chosen[R:]

    def spread(m, kind):
        block = xall.at[token_rows(m, bc(m), odd(m) + kind - 2 * odd(m) * kind)]
        for way, step in ((0, 1), (1, S - 1)):
            push(block, block, send.at[5], x2.at[(m * 2 + kind) * 4 + way], along_b(m, step)).start()

    def spread_on(m, kind):
        p = odd(m) + kind - 2 * odd(m) * kind
        for way, step in ((0, 1), (1, S - 1)):
            block = xall.at[token_rows(m, lax.rem(bc(m) + S - step, S), p)]
            arrived(block, x2.at[(m * 2 + kind) * 4 + way])
            push(
                block.at[way], block.at[way], send.at[0], x2.at[(m * 2 + kind) * 4 + 2 + way],
                along_b(m, step),
            ).start()

    def spread_end(m, kind):
        p = odd(m) + kind - 2 * odd(m) * kind
        block = xall.at[token_rows(m, lax.rem(bc(m) + 2, S), p)]
        for way in range(2):
            arrived(block.at[way], x2.at[(m * 2 + kind) * 4 + 2 + way])

    def both(step, *rest):
        @pl.loop(0, 2)
        def _(m):
            step(m, *rest)

    @pl.loop(0, 2)
    def _(m):
        mine = token_rows(m, bc(m), odd(m))
        push(xs.at[m * 2 + 1 - odd(m)], xall.at[mine], send.at[4], x1.at[m], mate(m)).start()
        xall[mine] = xs[m * 2 + odd(m)]
        spread(m, 0)

    @pl.loop(0, 2)
    def _(m):
        other = 1 - group(m)
        block = w_at(m, other, z, core)
        arrived(block, wx.at[m])
        ring_w(1, m, other)
        push(block, block, send.at[1], w2.at[(m * 2 + other) * NZ + z], partner).start()

    def pass_on_grads(j):
        @pl.loop(0, 2)
        def _(m):
            block = gall.at[token_rows(m, lax.rem(bc(m) + S - j, S), odd(m))]
            arrived(block, g1.at[m * S + j])
            push(block, block, send.at[3], g2.at[m * S + j], mate(m)).start()

    def ring_w_on(t, kind):
        @pl.loop(0, 2)
        def _(m):
            g = group(m) + kind - 2 * group(m) * kind
            ring_w_came(t, m, g)
            if t < H:
                ring_w(t + 1, m, g)

    loads[0].wait()
    loads[1].wait()
    ring_w_on(1, 0)
    pass_on_grads(1)
    pass_on_grads(3)
    pass_on_grads(2)
    ring_w_on(1, 1)

    @pl.loop(0, 2)
    def _(m):
        arrived(xall.at[token_rows(m, bc(m), 1 - odd(m))], x1.at[m])
        spread(m, 1)

    if H > 1:
        ring_w_on(2, 0)
    both(spread_on, 0)
    if H > 1:
        ring_w_on(2, 1)
    for t in range(3, H):
        ring_w_on(t, 0)
    both(spread_on, 1)
    for t in range(3, H):
        ring_w_on(t, 1)
    def rows_complete(m):
        spread_end(m, 0)
        spread_end(m, 1)

        @pl.loop(0, S)
        def _(j):
            b = lax.rem(bc(m) + S - j, S)
            arrived(gall.at[token_rows(m, b, 1 - odd(m))], g2.at[m * S + j])

    def lane_of(i):
        m, far = lax.div(jnp.int32(i), 2), 1 - lax.rem(jnp.int32(i), 2)
        g = group(m) + (1 - 2 * group(m)) * far
        return m, g, m * 2 + g

    def weight_grad(m, first_offset, tiles):
        @pl.loop(0, tiles)
        def _(n):
            zq = lax.rem(zl + first_offset + n * (ZL - 2), ZL)
            at = pl.ds(pl.multiple_of(zq * CH, CH), CH)
            left = jnp.concatenate(
                [xall[pl.ds(m * 2 * S, 2 * S), g, :, at].reshape(2 * S * R, CH) for g in range(2)], axis=1
            )
            for half in range(2):
                right = gall[pl.ds(m * 2 * S, 2 * S), :, half * WC:(half + 1) * WC]
                work[:, half * WC:(half + 1) * WC] = dot_tn(left, right.reshape(2 * S * R, WC))
            low = core == 0
            for g in range(2):
                top, mid, end = g * CH, g * CH + WR, (g + 1) * CH
                base = (m * 2 + g) * NZ + zq
                upper, lower = work[top:mid, :WC], work[mid:end, WC:]
                cross = (work[top:mid, WC:], work[mid:end, :WC])
                first = jnp.where(m == 0, cross[0], cross[1])
                second = jnp.where(m == 0, cross[1], cross[0])
                dw_own[base] = jnp.where(low, upper, first).astype(BF16)
                dw_own[base + ZL] = jnp.where(low, second, lower).astype(BF16)
                dw_peer[base] = jnp.where(low, first, upper).astype(BF16)
                dw_peer[base + ZL] = jnp.where(low, lower, second).astype(BF16)
                for part in range(2):
                    to = base + part * ZL
                    push(dw_peer.at[to], dw_sum.at[to], send.at[10], e1.at[to], partner).start()

    def share(lane, to):
        return dw_own[lane * NZ + to].astype(F32) + dw_sum[lane * NZ + to].astype(F32)

    def ring_start(lane):
        to = lax.rem(z + H, NZ)
        at = lane * NZ + to
        arrived(dw_sum.at[at], e1.at[at])
        dw_own[at] = share(lane, to).astype(BF16)
        for way, step in ((0, 1), (1, NZ - 1)):
            half = pl.ds(way * WH, WH)
            push(
                dw_own.at[at, half], ring.at[(way * H) * 4 + lane, half], send.at[6],
                e2.at[(way * H) * 4 + lane], along_z(step),
            ).start()

    def ring_step(t, lane):
        for way, step in ((0, 1), (1, NZ - 1)):
            to = lax.rem(z + step * (H - t), NZ)
            at = (way * H + t - 1) * 4 + lane
            arrived(dw_sum.at[lane * NZ + to], e1.at[lane * NZ + to])
            own = share(lane, to)
            if t == 1:
                half, rest = pl.ds(way * WH, WH), pl.ds((1 - way) * WH, WH)
                arrived(ring.at[at, half], e2.at[at])
                total = ring[at, half].astype(F32) + own[way * WH:(way + 1) * WH]
                ring[at, half] = total.astype(BF16)
                ring[at, rest] = own[(1 - way) * WH:(2 - way) * WH].astype(BF16)
            else:
                arrived(ring.at[at], e2.at[at])
                ring[at] = (ring[at].astype(F32) + own).astype(BF16)
            push(ring.at[at], ring.at[at + 4], send.at[11], e2.at[at + 4], along_z(step)).start()

    def ring_end(lane):
        arrived(dw_sum.at[lane * NZ + z], e1.at[lane * NZ + z])
        total = share(lane, z)
        for way in range(2):
            at = (way * H + H - 1) * 4 + lane
            if H == 1:
                half, rest = pl.ds(way * WH, WH), pl.ds((1 - way) * WH, WH)
                arrived(ring.at[at, half], e2.at[at])
                ring[at, rest] = jnp.zeros((WH, WC), BF16)
            else:
                arrived(ring.at[at], e2.at[at])
            total = total + ring[at].astype(F32)
        return total

    def queries(m):
        @pl.loop(0, S // 2)
        def _(i):
            base = token_rows(m, 2 * i, 0)
            for half in range(2):
                total = jnp.zeros((4 * R, WC), F32)
                for g in range(2):
                    block = xall[pl.ds(base, 4), g].reshape(4 * R, DS)
                    total = total + dot_nn(block, w[(m * 2 + g) * 2 + half])
                qp[pl.ds(base, 4), :, half * WC:(half + 1) * WC] = total.astype(BF16).reshape(4, R, WC)
            for n in range(2):
                b = 2 * i + n
                push(
                    qp.at[token_rows(m, b, 1 - odd(m))], qr.at[m * S + b], send.at[7],
                    q1.at[m * S + b], mate(m),
                ).start()

    def input_grads(m, first, second):
        bases = [token_rows(m, lax.rem(bc(m) + step, S), 0) for step in (first, second)]

        def taken(ref, *at):
            return jnp.concatenate([ref[(pl.ds(base, 2), *at)] for base in bases], axis=0)

        for g in range(2):
            for part in range(2):
                at = slice(part * (DS // 2), (part + 1) * (DS // 2))
                total = dot_nt(
                    taken(gall, slice(None), slice(0, WC)).reshape(4 * R, WC), w[(m * 2 + g) * 2, at, :]
                ) + dot_nt(
                    taken(gall, slice(None), slice(WC, ES)).reshape(4 * R, WC), w[(m * 2 + g) * 2 + 1, at, :]
                )
                short = total.astype(BF16).reshape(4, R, DS // 2)
                dp[pl.ds(bases[0], 2), g, :, at] = short[:2]
                dp[pl.ds(bases[1], 2), g, :, at] = short[2:]
                rowed = taken(xall, g, slice(None), at).reshape(4 * R, DS // 2).astype(F32)
                gacc[m * 2 + g, :, at] += jnp.sum(total * rowed, axis=0, keepdims=True)

    def rows_to(m, step):
        return pl.ds(token_rows(m, lax.rem(bc(m) + step, S), 0), 2)

    def grads_near(m, way, g):
        push(
            dp.at[rows_to(m, (1, S - 1)[way]), g], dr.at[pl.ds((m * 2 + way) * 2, 2), g],
            send.at[8], d1.at[(m * 2 + way) * 2 + g], along_b(m, (1, S - 1)[way]),
        ).start()

    def input_grads_first(m):
        input_grads(m, 2, 1)
        for way in range(2):
            push(
                dp.at[rows_to(m, 2), way], dm.at[pl.ds((m * 2 + way) * 2, 2)],
                send.at[22], d0.at[m * 2 + way], along_b(m, (1, S - 1)[way]),
            ).start()
        grads_near(m, 0, 1)

    def input_grads_last(m):
        input_grads(m, S - 1, 0)
        grads_near(m, 1, 0)

    def input_grads_mid(m):
        for way in range(2):
            came = dm.at[pl.ds((m * 2 + way) * 2, 2)]
            arrived(came, d0.at[m * 2 + way])
            at = rows_to(m, (1, S - 1)[way])
            dp[at, way] = (dp[at, way].astype(F32) + came[...].astype(F32)).astype(BF16)
            grads_near(m, way, way)

    def gain_step(m, came, slots, going, place_at):
        total = came[m * slots]
        for i in range(1, slots):
            total = total + came[m * slots + i]
        going[place_at] = total

    def gains_core():
        @pl.loop(0, 2)
        def _(m):
            for g in range(2):
                for i in range(GR):
                    g_core[m * 2 + core, g * GR + i:g * GR + i + 1, :] = gacc[
                        m * 2 + g, :, i * 128:(i + 1) * 128
                    ]
            mine = g_core.at[m * 2 + core]
            push(mine, mine, send.at[9], s1.at[m], partner).start()

    def gains_b():
        @pl.loop(0, 2)
        def _(m):
            arrived(g_core.at[m * 2 + 1 - core], s1.at[m])
            gain_step(m, g_core, 2, g_b, m * S + bc(m))
            mine = g_b.at[m * S + bc(m)]

            @pl.loop(1, S)
            def _(j):
                push(mine, mine, send.at[12], s2.at[m * S + j], along_b(m, j)).start()

    def gains_z():
        @pl.loop(0, 2)
        def _(m):
            @pl.loop(1, S)
            def _(j):
                arrived(g_b.at[m * S + lax.rem(bc(m) + S - j, S)], s2.at[m * S + j])

            gain_step(m, g_b, S, g_z, m * NZ + z)
            mine = g_z.at[m * NZ + z]

            @pl.loop(1, NZ)
            def _(k):
                push(mine, mine, send.at[13], s3.at[m * NZ + k], along_z(k)).start()

    def gains_c():
        @pl.loop(0, 2)
        def _(m):
            @pl.loop(1, NZ)
            def _(k):
                arrived(g_z.at[m * NZ + lax.rem(z + NZ - k, NZ)], s3.at[m * NZ + k])

            gain_step(m, g_z, NZ, g_c, m * S + cc(m))
            mine = g_c.at[m * S + cc(m)]

            @pl.loop(1, S)
            def _(k):
                push(mine, mine, send.at[14], s4.at[m * S + k], along_c(m, k)).start()

    def query_sums(m):
        @pl.loop(1, S + 1)
        def _(j):
            b = lax.rem(bc(m) + j, S)
            mine = token_rows(m, b, odd(m))
            arrived(qr.at[m * S + b], q1.at[m * S + b])
            total = (qp[mine].astype(F32) + qr[m * S + b].astype(F32)).astype(BF16)

            @pl.when(j < S)
            def _():
                qp[mine] = total
                push(
                    qp.at[mine], qf.at[m * S + bc(m)], send.at[15], q2.at[m * S + j], along_b(m, j)
                ).start()

            @pl.when(j == S)
            def _():
                qf[m * S + bc(m)] = total

    def grad_sums(m):
        for way in range(2):
            for g in range(2):
                arrived(dr.at[pl.ds((m * 2 + way) * 2, 2), g], d1.at[(m * 2 + way) * 2 + g])

        def summed(p, g):
            total = dp[token_rows(m, bc(m), p), g].astype(F32)
            for way in range(2):
                total = total + dr[(m * 2 + way) * 2 + p, g].astype(F32)
            return total.astype(BF16)

        theirs = token_rows(m, bc(m), 1 - odd(m))
        for g in range(2):
            dp[theirs, g] = summed(1 - odd(m), g)
        push(dp.at[theirs], df.at[m * 2 + odd(m)], send.at[16], d2.at[m], mate(m)).start()
        for g in range(2):
            df[m * 2 + odd(m), g] = summed(odd(m), g)

    def steps(t, *lanes):
        if t < H:
            for lane in lanes:
                ring_step(t, lane_of(lane)[2])

    gacc[...] = jnp.zeros_like(gacc)
    def ring_starts(m):
        ring_start(lane_of(2 * m)[2])
        ring_start(lane_of(2 * m + 1)[2])

    rows_complete(0)
    weight_grad(0, 0, 1)
    ring_w_on(H, 0)
    ring_w_on(H, 1)
    rows_complete(1)
    weight_grad(1, 0, 1)
    ring_starts(0)

    @pl.loop(0, 4 * NZ)
    def _(i):
        lane, k = lax.div(i, NZ), lax.rem(i, NZ)
        m, g = lax.div(lane, 2), lax.rem(lane, 2)
        arrived(w_at(m, g, k, 1 - core), w2.at[lane * NZ + k])

    input_grads_first(0)
    ring_starts(1)
    input_grads_first(1)

    @pl.loop(0, 2)
    def _(m):
        weight_grad(m, 1, 2)
        ring_step(1, lane_of(2 * m)[2])
        ring_step(1, lane_of(2 * m + 1)[2])

    both(input_grads_last)
    gains_core()
    both(weight_grad, 2, 1)
    steps(2, 0, 1)
    both(input_grads_mid)
    gains_b()
    queries(0)
    steps(2, 2, 3)
    queries(1)
    steps(3, 0, 1)
    steps(3, 2, 3)
    gains_z()
    both(grad_sums)
    query_sums(0)
    query_sums(1)
    gains_c()

    @pl.loop(0, 2)
    def _(m):
        other = 1 - group(m)
        dw_x[m] = ring_end(m * 2 + other).astype(BF16)
        push(dw_x.at[m], dw_xr.at[m], send.at[20], e3.at[m], twin(m)).start()

    stores = [
        pltpu.make_async_copy(cot_ref, q_out, local.at[0]),
        pltpu.make_async_copy(tok_ref, tg_out, local.at[1]),
        pltpu.make_async_copy(dw_end.at[0], dwt_out, local.at[2]),
        pltpu.make_async_copy(dw_end.at[1], dwi_out, local.at[3]),
        pltpu.make_async_copy(gain_ref.at[0], ggt_out, local.at[4]),
        pltpu.make_async_copy(gain_ref.at[1], ggi_out, local.at[5]),
    ]
    @pl.loop(0, 2)
    def _(m):
        arrived(df.at[m * 2 + 1 - odd(m)], d2.at[m])

    products = jnp.zeros((T, CH), F32)
    for c in range(S):
        half, g = c % 2, c // 2
        normed_grad = dot_nn(place[0], df[half, g]) + dot_nn(place[1], df[2 + half, g])
        for zq in range(ZL):
            at = slice(zq * S * CH + c * CH, zq * S * CH + (c + 1) * CH)
            gains = jnp.where(flag[...] > 0.5, gt_ref[:, at], gi_ref[:, at])
            part = normed_grad[:, zq * CH:(zq + 1) * CH] * gains
            grads[:, at] = part
            products = products + part * tok_ref[:, at].astype(F32)
    scale = inv[...]
    along = jnp.sum(products, axis=1, keepdims=True) / D * scale * scale
    for i in range(S * ZL):
        at = slice(i * CH, (i + 1) * CH)
        tok_ref[:, at] = (scale * (grads[:, at] - tok_ref[:, at].astype(F32) * along)).astype(BF16)

    stores[1].start()

    @pl.loop(0, 2)
    def _(m):
        @pl.loop(1, S)
        def _(j):
            arrived(qf.at[m * S + lax.rem(bc(m) + S - j, S)], q2.at[m * S + j])

    @pl.loop(0, S)
    def _(b):
        full = dot_nn(place[0], qf[b]) + dot_nn(place[1], qf[S + b])
        cot_ref[:, pl.ds(pl.multiple_of(b * ES, ES), ES)] = full.astype(BF16)

    stores[0].start()

    @pl.loop(0, 2)
    def _(m):
        @pl.loop(1, S)
        def _(k):
            arrived(g_c.at[m * S + lax.rem(cc(m) + S - k, S)], s4.at[m * S + k])

    for m, gain in ((0, gt_ref), (1, gi_ref)):
        for half in range(2):
            total = g_c[m * S + half]
            for k in range(half + 2, S, 2):
                total = total + g_c[m * S + k]
            for g in range(S // 2):
                for i in range(GR):
                    zq, off = (i * 128) // CH, (i * 128) % CH
                    first = zq * S * CH + (half + 2 * g) * CH + off
                    at = slice(first, first + 128)
                    gain_ref[m, :, at] = total[g * GR + i:g * GR + i + 1, :] / gain[:, at]

    stores[4].start()
    stores[5].start()

    @pl.loop(0, 2)
    def _(m):
        own = ring_end(m * 2 + group(m))
        arrived(dw_xr.at[m], e3.at[m])
        dw_end[m] = own + dw_xr[m].astype(F32)

    stores[2].start()
    stores[3].start()

    sent(w.at[pl.ds(0, 4)], send.at[1])
    sent(gs.at[pl.ds(0, 2 * (S - 1))], send.at[2])
    sent(gall.at[pl.ds(0, 2 * S)], send.at[3])
    sent(xs.at[pl.ds(0, 2)], send.at[4])
    sent(xall.at[pl.ds(0, 8)], send.at[5])
    sent(xall.at[pl.ds(0, 4)], send.at[0])
    sent(dw_own.at[pl.ds(0, 4)], send.at[6])
    sent(qp.at[pl.ds(0, 2 * S)], send.at[7])
    sent(dp.at[pl.ds(0, 8)], send.at[8])
    sent(dp.at[pl.ds(0, 4)], send.at[22])
    sent(g_core.at[pl.ds(0, 2)], send.at[9])
    sent(dw_peer, send.at[10])
    if H > 1:
        sent(ring.at[pl.ds(0, 8 * (H - 1))], send.at[11])
    sent(g_b.at[pl.ds(0, 2 * (S - 1))], send.at[12])
    sent(g_z.at[pl.ds(0, 2 * (NZ - 1))], send.at[13])
    sent(g_c.at[pl.ds(0, 2 * (S - 1))], send.at[14])
    sent(qp.at[pl.ds(0, 2 * (S - 1))], send.at[15])
    sent(dp.at[pl.ds(0, 2)], send.at[16])
    sent(dw_x, send.at[17])
    if H > 1:
        sent(ring.at[pl.ds(0, 8 * (H - 1))], send.at[18])
    sent(dw_own.at[pl.ds(0, 4)], send.at[19])
    sent(dw_x, send.at[20])
    for store in stores:
        store.wait()


def hand_on(*refs):
    came, gone = refs[-2:]
    count = (len(refs) - 2) // 3
    loads, stores = [], []
    for i in range(count):
        rows = refs[i].shape[0]
        step = max(rows // 4, 1)
        for first in range(0, rows, step):
            at, sem = pl.ds(first, step), len(loads)
            held = refs[2 * count + i].at[at]
            loads.append(pltpu.make_async_copy(refs[i].at[at], held, came.at[sem]))
            stores.append(pltpu.make_async_copy(held, refs[count + i].at[at], gone.at[sem]))
    for load in loads:
        load.start()
    for load, store in zip(loads, stores):
        load.wait()
        store.start()
    for store in stores:
        store.wait()


def solution(mesh):
    ZL, S = mesh.shape["dp"], mesh.shape["text"] // 2
    NZ = 2 * ZL
    H = NZ // 2

    def shards(tokens, modality, gain_text, gain_image, text_weight, image_weight, cotangent):
        T, D = tokens.shape
        E = cotangent.shape[1]
        R = -(-min(CAP, T) // 16) * 16
        DS, ES = D // S, E // S
        CH = DS // ZL
        WR, WC = CH // 2, ES // 2
        GR = DS // 128
        vmem = pl.BlockSpec(memory_space=pltpu.VMEM)
        dma = pltpu.SemaphoreType.DMA
        dims = (S, ZL, T, R, DS, ES)
        anywhere = pl.BlockSpec(memory_space=pl.ANY)
        modality, gain_text, gain_image = (
            modality.reshape(1, T), gain_text.reshape(1, D), gain_image.reshape(1, D)
        )
        shapes = (
            jax.ShapeDtypeStruct((T, E), BF16),
            jax.ShapeDtypeStruct((T, D), BF16),
            jax.ShapeDtypeStruct((WR, WC), F32),
            jax.ShapeDtypeStruct((WR, WC), F32),
            jax.ShapeDtypeStruct((1, D), F32),
            jax.ShapeDtypeStruct((1, D), F32),
        )
        parts = pl.pallas_call(
            functools.partial(layer, dims),
            out_shape=shapes,
            in_specs=[vmem] * 3 + [anywhere] * 4,
            out_specs=(anywhere,) * 6,
            scratch_shapes=[
                pltpu.VMEM((T, D), BF16),
                pltpu.VMEM((T, E), BF16),
                pltpu.VMEM((2 * R, T), BF16),
                pltpu.VMEM((2, T, R), BF16),
                pltpu.VMEM((T, 1), F32),
                pltpu.VMEM((T, 1), F32),
                pltpu.VMEM((2 * CH, ES), F32),
                pltpu.VMEM((T, D), F32),
                pltpu.VMEM((4, 1, DS), F32),
                pltpu.VMEM((4, 2, R, DS), BF16),
                pltpu.VMEM((2 * S, R, ES), BF16),
                pltpu.VMEM((4 * S, 2, R, DS), BF16),
                pltpu.VMEM((4 * S, R, ES), BF16),
                pltpu.VMEM((8, DS, WC), BF16),
                pltpu.VMEM((4 * S, R, ES), BF16),
                pltpu.VMEM((4 * S, 2, R, DS), BF16),
                pltpu.VMEM((2 * S, R, ES), BF16),
                pltpu.VMEM((8, R, DS), BF16),
                pltpu.VMEM((8, 2, R, DS), BF16),
                pltpu.VMEM((2 * S, R, ES), BF16),
                pltpu.VMEM((4, 2, R, DS), BF16),
                pltpu.VMEM((4 * NZ, WR, WC), BF16),
                pltpu.VMEM((4 * NZ, WR, WC), BF16),
                pltpu.VMEM((4 * NZ, WR, WC), BF16),
                pltpu.VMEM((8 * H, WR, WC), BF16),
                pltpu.VMEM((2, WR, WC), BF16),
                pltpu.VMEM((2, WR, WC), BF16),
                pltpu.VMEM((2, WR, WC), F32),
                pltpu.VMEM((4, 2 * GR, 128), F32),
                pltpu.VMEM((2 * S, 2 * GR, 128), F32),
                pltpu.VMEM((2 * NZ, 2 * GR, 128), F32),
                pltpu.VMEM((2 * S, 2 * GR, 128), F32),
                pltpu.VMEM((2, 1, D), F32),
                dma((6,)),
                dma((23,)),
                dma((2,)),
                dma((16,)),
                dma((2 * S,)),
                dma((2 * S,)),
                dma((2,)),
                dma((8 * H,)),
                dma((4 * NZ,)),
                dma((2 * S,)),
                dma((2 * S,)),
                dma((4,)),
                dma((8,)),
                dma((2,)),
                dma((4 * NZ,)),
                dma((8 * H,)),
                dma((2,)),
                dma((2,)),
                dma((2 * S,)),
                dma((2 * NZ,)),
                dma((2 * S,)),
            ],
            compiler_params=pltpu.CompilerParams(
                collective_id=0, has_side_effects=True, vmem_limit_bytes=60 * 2**20
            ),
        )(modality, gain_text, gain_image, tokens, cotangent, text_weight, image_weight)
        outs = pl.pallas_call(
            hand_on,
            out_shape=shapes,
            in_specs=[anywhere] * 6,
            out_specs=(anywhere,) * 6,
            scratch_shapes=[pltpu.VMEM(a.shape, a.dtype) for a in shapes] + [dma((18,)), dma((18,))],
            compiler_params=pltpu.CompilerParams(vmem_limit_bytes=60 * 2**20),
        )(*parts)
        return (*outs[:4], outs[4].reshape(D), outs[5].reshape(D))

    rows = P(("dp", "text", "image"), None)
    text_at, image_at = P(("dp", "image"), "text"), P(("dp", "text"), "image")
    return jax.shard_map(
        shards,
        mesh=mesh,
        in_specs=(rows, P(("dp", "text", "image")), P(), P(), text_at, image_at, rows),
        out_specs=(rows, rows, text_at, image_at, P(), P()),
        check_vma=False,
    )
```

```python
import functools

import jax
import jax.numpy as jnp
from jax import lax
from jax.experimental import pallas as pl
from jax.experimental.pallas import tpu as pltpu
from jax.sharding import PartitionSpec as P

MESH = pl.DeviceIdType.MESH
CAP = 72
EPSILON = 1e-05
F32 = jnp.float32
BF16 = jnp.bfloat16


def dot_nn(left, right):
    return jnp.dot(left, right, preferred_element_type=F32)


def dot_nt(left, right):
    return lax.dot_general(left, right, (((1,), (1,)), ((), ())), preferred_element_type=F32)


def dot_tn(left, right):
    return lax.dot_general(left, right, (((0,), (0,)), ((), ())), preferred_element_type=F32)


def ranks(modality, T):
    rows = lax.broadcasted_iota(jnp.int32, (T, T), 0)
    cols = lax.broadcasted_iota(jnp.int32, (T, T), 1)
    flag_row = jnp.where(modality == 0, 1.0, 0.0)
    wide = jnp.broadcast_to(flag_row, (T, T))
    flag_col = jnp.sum(jnp.where(rows == cols, wide, 0.0), axis=1, keepdims=True)
    rank_col = jnp.sum(jnp.where(cols < rows, wide, 0.0), axis=1, keepdims=True)
    tall = jnp.broadcast_to(flag_col, (T, T))
    rank_row = jnp.sum(jnp.where(rows < cols, tall, 0.0), axis=0, keepdims=True)
    return flag_row, flag_col, rank_row, rank_col


def layer(
    dims,
    mod_ref, gt_ref, gi_ref, tok_in, cot_in, wt_in, wi_in,
    q_out, tg_out, dwt_out, dwi_out, ggt_out, ggi_out,
    tok_ref, cot_ref, pick, place, flag, inv, work, grads, gacc,
    xs, gs, xall, gall, w, qp, dp, qr, dm, dr, qf, df,
    dw_own, dw_peer, dw_sum, ring, dw_x, dw_xr, dw_end,
    g_core, g_b, g_z, g_c, gain_ref,
    local, send, x1, x2, g1, g2, wx, w1, w2, q1, q2, d0, d1, d2, e1, e2, e3, s1, s2, s3, s4,
):
    S, ZL, T, R, DS, ES = dims
    NZ = 2 * ZL
    H = NZ // 2
    CH = DS // ZL
    WR, WC = CH // 2, ES // 2
    WH = WR // 2
    D, E = DS * S, ES * S
    GR = DS // 128
    zl, text, image = lax.axis_index("dp"), lax.axis_index("text"), lax.axis_index("image")
    y, core = lax.div(text, 2), lax.rem(text, 2)
    x, zh = lax.div(image, 2), lax.rem(image, 2)
    z = zh * ZL + zl

    def cc(m):
        return x + (y - x) * m

    def bc(m):
        return y + (x - y) * m

    def odd(m):
        return lax.rem(cc(m), 2)

    def along_c(m, k):
        return (zl, lax.rem(text + 2 * k * m, 2 * S), lax.rem(image + 2 * k * (1 - m), 2 * S))

    def along_b(m, k):
        return (zl, lax.rem(text + 2 * k * (1 - m), 2 * S), lax.rem(image + 2 * k * m, 2 * S))

    def along_z(k):
        to = lax.rem(z + k, NZ)
        return (lax.rem(to, ZL), text, 2 * x + lax.div(to, ZL))

    def mate(m):
        return along_c(m, 1 + (S - 2) * lax.rem(cc(m) + core, 2))

    def twin(m):
        return along_c(m, 2)

    partner = (zl, text + 1 - 2 * core, image)

    def push(src, dst, send_sem, recv_sem, device):
        return pltpu.make_async_remote_copy(
            src_ref=src, dst_ref=dst, send_sem=send_sem, recv_sem=recv_sem,
            device_id=device, device_id_type=MESH,
        )

    def arrived(dst, recv_sem):
        push(dst, dst, send.at[21], recv_sem, partner).wait_recv()

    def sent(src, send_sem):
        push(src, src, send_sem, q1.at[0], partner).wait_send()

    barrier = pltpu.get_barrier_semaphore()

    @pl.loop(1, S)
    def _(k):
        pl.semaphore_signal(barrier, inc=1, device_id=along_c(0, k), device_id_type=MESH)
        pl.semaphore_signal(barrier, inc=1, device_id=along_b(0, k), device_id_type=MESH)

    @pl.loop(1, NZ)
    def _(k):
        pl.semaphore_signal(barrier, inc=1, device_id=along_z(k), device_id_type=MESH)

    pl.semaphore_signal(barrier, inc=1, device_id=partner, device_id_type=MESH)

    def w_at(m, g, from_z, from_core, part=None):
        from_zh, from_zl = lax.div(from_z, ZL), lax.rem(from_z, ZL)
        half = from_core + (from_zh - from_core) * m
        row = 2 * from_zl + from_zh + (from_core - from_zh) * m
        if part is None:
            at = pl.ds(pl.multiple_of(row * WR, WR), WR)
        else:
            at = pl.ds(pl.multiple_of(row * WR + part * WH, WH), WH)
        return w.at[(m * 2 + g) * 2 + half, at, :]

    def group(m):
        return lax.div(cc(m), 2)

    loads = [
        pltpu.make_async_copy(wt_in, w_at(0, group(0), z, core), local.at[0]),
        pltpu.make_async_copy(wi_in, w_at(1, group(1), z, core), local.at[1]),
        pltpu.make_async_copy(cot_in, cot_ref, local.at[2]),
        pltpu.make_async_copy(tok_in, tok_ref, local.at[3]),
    ]
    for load in loads:
        load.start()

    def ring_w(t, m, g):
        lane = m * 2 + g
        if t < H:
            for way, step in ((0, 1), (1, NZ - 1)):
                block = w_at(m, g, lax.rem(z + (NZ - step) * (t - 1), NZ), core)
                push(block, block, send.at[18], w1.at[(way * H + t - 1) * 4 + lane], along_z(step)).start()
        else:
            for way, step in ((0, 1), (1, NZ - 1)):
                block = w_at(m, g, lax.rem(z + (NZ - step) * (t - 1), NZ), core, way)
                push(block, block, send.at[19], w1.at[(way * H + t - 1) * 4 + lane], along_z(step)).start()

    def ring_w_came(t, m, g):
        lane = m * 2 + g
        for way, step in ((0, 1), (1, NZ - 1)):
            origin = lax.rem(z + (NZ - step) * t, NZ)
            if t < H:
                block = w_at(m, g, origin, core)
                arrived(block, w1.at[(way * H + t - 1) * 4 + lane])
                push(block, block, send.at[1], w2.at[lane * NZ + origin], partner).start()
            else:
                arrived(w_at(m, g, origin, core, way), w1.at[(way * H + t - 1) * 4 + lane])
        if t == H:
            block = w_at(m, g, lax.rem(z + H, NZ), core)
            push(block, block, send.at[1], w2.at[lane * NZ + lax.rem(z + H, NZ)], partner).start()

    pl.semaphore_wait(barrier, 2 * (S - 1) + NZ)
    for m, mine in ((0, wt_in), (1, wi_in)):
        lane = m * 2 + group(m)
        place_at = w_at(m, group(m), z, core)
        for way, step in ((0, 1), (1, NZ - 1)):
            push(mine, place_at, send.at[18], w1.at[way * H * 4 + lane], along_z(step)).start()
        push(mine, place_at, send.at[17], wx.at[m], twin(m)).start()
        push(mine, place_at, send.at[1], w2.at[lane * NZ + z], partner).start()

    flag_row, flag_col, rank_row, rank_col = ranks(mod_ref[...], T)
    flag[...] = flag_col
    slot = lax.broadcasted_iota(jnp.int32, (R, T), 0).astype(F32)
    spot = lax.broadcasted_iota(jnp.int32, (R, T), 1).astype(F32)
    pick[:R] = jnp.where((rank_row == slot) & (flag_row > 0.5), 1.0, 0.0).astype(BF16)
    pick[R:] = jnp.where((spot - rank_row == slot) & (flag_row < 0.5), 1.0, 0.0).astype(BF16)

    slot = lax.broadcasted_iota(jnp.int32, (T, R), 1).astype(F32)
    spot = lax.broadcasted_iota(jnp.int32, (T, R), 0).astype(F32)
    place[0] = jnp.where((rank_col == slot) & (flag_col > 0.5), 1.0, 0.0).astype(BF16)
    place[1] = jnp.where((spot - rank_col == slot) & (flag_col < 0.5), 1.0, 0.0).astype(BF16)

    loads[2].wait()

    @pl.loop(0, S)
    def _(b):
        part = cot_ref[:, pl.ds(pl.multiple_of(b * ES, ES), ES)]
        chosen = dot_nn(pick[...], part).astype(BF16)
        gs[b] = chosen[:R]
        gs[S + b] = chosen[R:]

    def token_rows(m, b, p):
        return (m * S + b) * 2 + p

    @pl.loop(0, 2)
    def _(m):
        mine = token_rows(m, bc(m), odd(m))
        gall[mine] = gs[m * S + bc(m)]

        @pl.loop(1, S)
        def _(j):
            to = lax.rem(bc(m) + j, S)
            push(gs.at[m * S + to], gall.at[mine], send.at[2], g1.at[m * S + j], along_b(m, j)).start()

        push(gall.at[mine], gall.at[mine], send.at[3], g2.at[m * S], mate(m)).start()

    loads[3].wait()
    squares = jnp.zeros((T, CH), F32)
    for i in range(S * ZL):
        part = tok_ref[:, i * CH:(i + 1) * CH].astype(F32)
        squares = squares + part * part
    inv[...] = lax.rsqrt(jnp.sum(squares, axis=1, keepdims=True) / D + EPSILON)

    scale = jnp.broadcast_to(inv[...], (T, CH))
    is_text = jnp.broadcast_to(flag[...], (T, CH)) > 0.5

    @pl.loop(0, S)
    def _(c):
        half, g = lax.rem(c, 2), lax.div(c, 2)
        for zq in range(ZL):
            at = pl.ds(pl.multiple_of(zq * (S * CH) + c * CH, CH), CH)
            gains = jnp.where(is_text, gt_ref[:, at], gi_ref[:, at])
            normed = (tok_ref[:, at].astype(F32) * scale * gains).astype(BF16)
            chosen = dot_nn(pick[...], normed).astype(BF16)
            xs[half, g, :, zq * CH:(zq + 1) * CH] = chosen[:R]
            xs[2 + half, g, :, zq * CH:(zq + 1) * CH] = chosen[R:]

    def spread(m, kind):
        block = xall.at[token_rows(m, bc(m), odd(m) + kind - 2 * odd(m) * kind)]
        for way, step in ((0, 1), (1, S - 1)):
            push(block, block, send.at[5], x2.at[(m * 2 + kind) * 4 + way], along_b(m, step)).start()

    def spread_on(m, kind):
        p = odd(m) + kind - 2 * odd(m) * kind
        for way, step in ((0, 1), (1, S - 1)):
            block = xall.at[token_rows(m, lax.rem(bc(m) + S - step, S), p)]
            arrived(block, x2.at[(m * 2 + kind) * 4 + way])
            push(
                block.at[way], block.at[way], send.at[0], x2.at[(m * 2 + kind) * 4 + 2 + way],
                along_b(m, step),
            ).start()

    def spread_end(m, kind):
        p = odd(m) + kind - 2 * odd(m) * kind
        block = xall.at[token_rows(m, lax.rem(bc(m) + 2, S), p)]
        for way in range(2):
            arrived(block.at[way], x2.at[(m * 2 + kind) * 4 + 2 + way])

    def both(step, *rest):
        @pl.loop(0, 2)
        def _(m):
            step(m, *rest)

    @pl.loop(0, 2)
    def _(m):
        mine = token_rows(m, bc(m), odd(m))
        push(xs.at[m * 2 + 1 - odd(m)], xall.at[mine], send.at[4], x1.at[m], mate(m)).start()
        xall[mine] = xs[m * 2 + odd(m)]
        spread(m, 0)

    @pl.loop(0, 2)
    def _(m):
        other = 1 - group(m)
        block = w_at(m, other, z, core)
        arrived(block, wx.at[m])
        ring_w(1, m, other)
        push(block, block, send.at[1], w2.at[(m * 2 + other) * NZ + z], partner).start()

    def pass_on_grads(j):
        @pl.loop(0, 2)
        def _(m):
            block = gall.at[token_rows(m, lax.rem(bc(m) + S - j, S), odd(m))]
            arrived(block, g1.at[m * S + j])
            push(block, block, send.at[3], g2.at[m * S + j], mate(m)).start()

    def ring_w_on(t, kind):
        @pl.loop(0, 2)
        def _(m):
            g = group(m) + kind - 2 * group(m) * kind
            ring_w_came(t, m, g)
            if t < H:
                ring_w(t + 1, m, g)

    loads[0].wait()
    loads[1].wait()
    ring_w_on(1, 0)
    pass_on_grads(1)
    pass_on_grads(3)
    pass_on_grads(2)
    ring_w_on(1, 1)

    @pl.loop(0, 2)
    def _(m):
        arrived(xall.at[token_rows(m, bc(m), 1 - odd(m))], x1.at[m])
        spread(m, 1)

    if H > 1:
        ring_w_on(2, 0)
    both(spread_on, 0)
    if H > 1:
        ring_w_on(2, 1)
    for t in range(3, H):
        ring_w_on(t, 0)
    both(spread_on, 1)
    for t in range(3, H):
        ring_w_on(t, 1)
    def rows_complete(m):
        spread_end(m, 0)
        spread_end(m, 1)

        @pl.loop(0, S)
        def _(j):
            b = lax.rem(bc(m) + S - j, S)
            arrived(gall.at[token_rows(m, b, 1 - odd(m))], g2.at[m * S + j])

    def lane_of(i):
        m, far = lax.div(jnp.int32(i), 2), 1 - lax.rem(jnp.int32(i), 2)
        g = group(m) + (1 - 2 * group(m)) * far
        return m, g, m * 2 + g

    def weight_grad(m, first_offset, tiles):
        @pl.loop(0, tiles)
        def _(n):
            zq = lax.rem(zl + first_offset + n * (ZL - 2), ZL)
            at = pl.ds(pl.multiple_of(zq * CH, CH), CH)
            left = jnp.concatenate(
                [xall[pl.ds(m * 2 * S, 2 * S), g, :, at].reshape(2 * S * R, CH) for g in range(2)], axis=1
            )
            for half in range(2):
                right = gall[pl.ds(m * 2 * S, 2 * S), :, half * WC:(half + 1) * WC]
                work[:, half * WC:(half + 1) * WC] = dot_tn(left, right.reshape(2 * S * R, WC))
            low = core == 0
            for g in range(2):
                top, mid, end = g * CH, g * CH + WR, (g + 1) * CH
                base = (m * 2 + g) * NZ + zq
                upper, lower = work[top:mid, :WC], work[mid:end, WC:]
                cross = (work[top:mid, WC:], work[mid:end, :WC])
                first = jnp.where(m == 0, cross[0], cross[1])
                second = jnp.where(m == 0, cross[1], cross[0])
                dw_own[base] = jnp.where(low, upper, first).astype(BF16)
                dw_own[base + ZL] = jnp.where(low, second, lower).astype(BF16)
                dw_peer[base] = jnp.where(low, first, upper).astype(BF16)
                dw_peer[base + ZL] = jnp.where(low, lower, second).astype(BF16)
                for part in range(2):
                    to = base + part * ZL
                    push(dw_peer.at[to], dw_sum.at[to], send.at[10], e1.at[to], partner).start()

    def share(lane, to):
        return dw_own[lane * NZ + to].astype(F32) + dw_sum[lane * NZ + to].astype(F32)

    def ring_start(lane):
        to = lax.rem(z + H, NZ)
        at = lane * NZ + to
        arrived(dw_sum.at[at], e1.at[at])
        dw_own[at] = share(lane, to).astype(BF16)
        for way, step in ((0, 1), (1, NZ - 1)):
            half = pl.ds(way * WH, WH)
            push(
                dw_own.at[at, half], ring.at[(way * H) * 4 + lane, half], send.at[6],
                e2.at[(way * H) * 4 + lane], along_z(step),
            ).start()

    def ring_step(t, lane):
        for way, step in ((0, 1), (1, NZ - 1)):
            to = lax.rem(z + step * (H - t), NZ)
            at = (way * H + t - 1) * 4 + lane
            arrived(dw_sum.at[lane * NZ + to], e1.at[lane * NZ + to])
            own = share(lane, to)
            if t == 1:
                half, rest = pl.ds(way * WH, WH), pl.ds((1 - way) * WH, WH)
                arrived(ring.at[at, half], e2.at[at])
                total = ring[at, half].astype(F32) + own[way * WH:(way + 1) * WH]
                ring[at, half] = total.astype(BF16)
                ring[at, rest] = own[(1 - way) * WH:(2 - way) * WH].astype(BF16)
            else:
                arrived(ring.at[at], e2.at[at])
                ring[at] = (ring[at].astype(F32) + own).astype(BF16)
            push(ring.at[at], ring.at[at + 4], send.at[11], e2.at[at + 4], along_z(step)).start()

    def ring_end(lane):
        arrived(dw_sum.at[lane * NZ + z], e1.at[lane * NZ + z])
        total = share(lane, z)
        for way in range(2):
            at = (way * H + H - 1) * 4 + lane
            if H == 1:
                half, rest = pl.ds(way * WH, WH), pl.ds((1 - way) * WH, WH)
                arrived(ring.at[at, half], e2.at[at])
                ring[at, rest] = jnp.zeros((WH, WC), BF16)
            else:
                arrived(ring.at[at], e2.at[at])
            total = total + ring[at].astype(F32)
        return total

    def queries(m):
        @pl.loop(0, S // 2)
        def _(i):
            base = token_rows(m, 2 * i, 0)
            for half in range(2):
                total = jnp.zeros((4 * R, WC), F32)
                for g in range(2):
                    block = xall[pl.ds(base, 4), g].reshape(4 * R, DS)
                    total = total + dot_nn(block, w[(m * 2 + g) * 2 + half])
                qp[pl.ds(base, 4), :, half * WC:(half + 1) * WC] = total.astype(BF16).reshape(4, R, WC)
            for n in range(2):
                b = 2 * i + n
                push(
                    qp.at[token_rows(m, b, 1 - odd(m))], qr.at[m * S + b], send.at[7],
                    q1.at[m * S + b], mate(m),
                ).start()

    def input_grads(m, first, second):
        bases = [token_rows(m, lax.rem(bc(m) + step, S), 0) for step in (first, second)]

        def taken(ref, *at):
            return jnp.concatenate([ref[(pl.ds(base, 2), *at)] for base in bases], axis=0)

        for g in range(2):
            for part in range(2):
                at = slice(part * (DS // 2), (part + 1) * (DS // 2))
                total = dot_nt(
                    taken(gall, slice(None), slice(0, WC)).reshape(4 * R, WC), w[(m * 2 + g) * 2, at, :]
                ) + dot_nt(
                    taken(gall, slice(None), slice(WC, ES)).reshape(4 * R, WC), w[(m * 2 + g) * 2 + 1, at, :]
                )
                short = total.astype(BF16).reshape(4, R, DS // 2)
                dp[pl.ds(bases[0], 2), g, :, at] = short[:2]
                dp[pl.ds(bases[1], 2), g, :, at] = short[2:]
                rowed = taken(xall, g, slice(None), at).reshape(4 * R, DS // 2).astype(F32)
                gacc[m * 2 + g, :, at] += jnp.sum(total * rowed, axis=0, keepdims=True)

    def rows_to(m, step):
        return pl.ds(token_rows(m, lax.rem(bc(m) + step, S), 0), 2)

    def grads_near(m, way, g):
        push(
            dp.at[rows_to(m, (1, S - 1)[way]), g], dr.at[pl.ds((m * 2 + way) * 2, 2), g],
            send.at[8], d1.at[(m * 2 + way) * 2 + g], along_b(m, (1, S - 1)[way]),
        ).start()

    def input_grads_first(m):
        input_grads(m, 2, 1)
        for way in range(2):
            push(
                dp.at[rows_to(m, 2), way], dm.at[pl.ds((m * 2 + way) * 2, 2)],
                send.at[22], d0.at[m * 2 + way], along_b(m, (1, S - 1)[way]),
            ).start()
        grads_near(m, 0, 1)

    def input_grads_last(m):
        input_grads(m, S - 1, 0)
        grads_near(m, 1, 0)

    def input_grads_mid(m):
        for way in range(2):
            came = dm.at[pl.ds((m * 2 + way) * 2, 2)]
            arrived(came, d0.at[m * 2 + way])
            at = rows_to(m, (1, S - 1)[way])
            dp[at, way] = (dp[at, way].astype(F32) + came[...].astype(F32)).astype(BF16)
            grads_near(m, way, way)

    def gain_step(m, came, slots, going, place_at):
        total = came[m * slots]
        for i in range(1, slots):
            total = total + came[m * slots + i]
        going[place_at] = total

    def gains_core():
        @pl.loop(0, 2)
        def _(m):
            for g in range(2):
                for i in range(GR):
                    g_core[m * 2 + core, g * GR + i:g * GR + i + 1, :] = gacc[
                        m * 2 + g, :, i * 128:(i + 1) * 128
                    ]
            mine = g_core.at[m * 2 + core]
            push(mine, mine, send.at[9], s1.at[m], partner).start()

    def gains_b():
        @pl.loop(0, 2)
        def _(m):
            arrived(g_core.at[m * 2 + 1 - core], s1.at[m])
            gain_step(m, g_core, 2, g_b, m * S + bc(m))
            mine = g_b.at[m * S + bc(m)]

            @pl.loop(1, S)
            def _(j):
                push(mine, mine, send.at[12], s2.at[m * S + j], along_b(m, j)).start()

    def gains_z():
        @pl.loop(0, 2)
        def _(m):
            @pl.loop(1, S)
            def _(j):
                arrived(g_b.at[m * S + lax.rem(bc(m) + S - j, S)], s2.at[m * S + j])

            gain_step(m, g_b, S, g_z, m * NZ + z)
            mine = g_z.at[m * NZ + z]

            @pl.loop(1, NZ)
            def _(k):
                push(mine, mine, send.at[13], s3.at[m * NZ + k], along_z(k)).start()

    def gains_c():
        @pl.loop(0, 2)
        def _(m):
            @pl.loop(1, NZ)
            def _(k):
                arrived(g_z.at[m * NZ + lax.rem(z + NZ - k, NZ)], s3.at[m * NZ + k])

            gain_step(m, g_z, NZ, g_c, m * S + cc(m))
            mine = g_c.at[m * S + cc(m)]

            @pl.loop(1, S)
            def _(k):
                push(mine, mine, send.at[14], s4.at[m * S + k], along_c(m, k)).start()

    def query_sums(m):
        @pl.loop(1, S + 1)
        def _(j):
            b = lax.rem(bc(m) + j, S)
            mine = token_rows(m, b, odd(m))
            arrived(qr.at[m * S + b], q1.at[m * S + b])
            total = (qp[mine].astype(F32) + qr[m * S + b].astype(F32)).astype(BF16)

            @pl.when(j < S)
            def _():
                qp[mine] = total
                push(
                    qp.at[mine], qf.at[m * S + bc(m)], send.at[15], q2.at[m * S + j], along_b(m, j)
                ).start()

            @pl.when(j == S)
            def _():
                qf[m * S + bc(m)] = total

    def grad_sums(m):
        for way in range(2):
            for g in range(2):
                arrived(dr.at[pl.ds((m * 2 + way) * 2, 2), g], d1.at[(m * 2 + way) * 2 + g])

        def summed(p, g):
            total = dp[token_rows(m, bc(m), p), g].astype(F32)
            for way in range(2):
                total = total + dr[(m * 2 + way) * 2 + p, g].astype(F32)
            return total.astype(BF16)

        theirs = token_rows(m, bc(m), 1 - odd(m))
        for g in range(2):
            dp[theirs, g] = summed(1 - odd(m), g)
        push(dp.at[theirs], df.at[m * 2 + odd(m)], send.at[16], d2.at[m], mate(m)).start()
        for g in range(2):
            df[m * 2 + odd(m), g] = summed(odd(m), g)

    def steps(t, *lanes):
        if t < H:
            for lane in lanes:
                ring_step(t, lane_of(lane)[2])

    gacc[...] = jnp.zeros_like(gacc)
    def ring_starts(m):
        ring_start(lane_of(2 * m)[2])
        ring_start(lane_of(2 * m + 1)[2])

    rows_complete(0)
    weight_grad(0, 0, 1)
    ring_w_on(H, 0)
    ring_w_on(H, 1)
    rows_complete(1)
    weight_grad(1, 0, 1)
    ring_starts(0)

    @pl.loop(0, 4 * NZ)
    def _(i):
        lane, k = lax.div(i, NZ), lax.rem(i, NZ)
        m, g = lax.div(lane, 2), lax.rem(lane, 2)
        arrived(w_at(m, g, k, 1 - core), w2.at[lane * NZ + k])

    input_grads_first(0)
    ring_starts(1)
    input_grads_first(1)

    @pl.loop(0, 2)
    def _(m):
        weight_grad(m, 1, 2)
        ring_step(1, lane_of(2 * m)[2])
        ring_step(1, lane_of(2 * m + 1)[2])

    both(input_grads_last)
    gains_core()
    weight_grad(0, 2, 1)
    steps(2, 0, 1)
    both(input_grads_mid)
    weight_grad(1, 2, 1)
    gains_b()
    queries(0)
    steps(2, 2, 3)
    queries(1)
    steps(3, 0, 1)
    steps(3, 2)
    both(grad_sums)
    steps(3, 3)
    gains_z()
    query_sums(0)
    query_sums(1)
    gains_c()

    @pl.loop(0, 2)
    def _(m):
        other = 1 - group(m)
        dw_x[m] = ring_end(m * 2 + other).astype(BF16)
        push(dw_x.at[m], dw_xr.at[m], send.at[20], e3.at[m], twin(m)).start()

    stores = [
        pltpu.make_async_copy(cot_ref, q_out, local.at[0]),
        pltpu.make_async_copy(tok_ref, tg_out, local.at[1]),
        pltpu.make_async_copy(dw_end.at[0], dwt_out, local.at[2]),
        pltpu.make_async_copy(dw_end.at[1], dwi_out, local.at[3]),
        pltpu.make_async_copy(gain_ref.at[0], ggt_out, local.at[4]),
        pltpu.make_async_copy(gain_ref.at[1], ggi_out, local.at[5]),
    ]
    is_text = jnp.broadcast_to(flag[...], (T, CH)) > 0.5
    for i in range(S * ZL):
        at = slice(i * CH, (i + 1) * CH)
        grads[:, at] = jnp.where(is_text, gt_ref[:, at], gi_ref[:, at])

    @pl.loop(0, 2)
    def _(m):
        arrived(df.at[m * 2 + 1 - odd(m)], d2.at[m])

    products = jnp.zeros((T, CH), F32)
    for c in range(S):
        half, g = c % 2, c // 2
        normed_grad = dot_nn(place[0], df[half, g]) + dot_nn(place[1], df[2 + half, g])
        for zq in range(ZL):
            at = slice(zq * S * CH + c * CH, zq * S * CH + (c + 1) * CH)
            part = normed_grad[:, zq * CH:(zq + 1) * CH] * grads[:, at]
            grads[:, at] = part
            products = products + part * tok_ref[:, at].astype(F32)
    scale = inv[...]
    along = jnp.sum(products, axis=1, keepdims=True) / D * scale * scale
    scale, along = jnp.broadcast_to(scale, (T, CH)), jnp.broadcast_to(along, (T, CH))
    for i in range(S * ZL):
        at = slice(i * CH, (i + 1) * CH)
        tok_ref[:, at] = (scale * (grads[:, at] - tok_ref[:, at].astype(F32) * along)).astype(BF16)

    stores[1].start()

    @pl.loop(0, 2)
    def _(m):
        @pl.loop(1, S)
        def _(j):
            arrived(qf.at[m * S + lax.rem(bc(m) + S - j, S)], q2.at[m * S + j])

    @pl.loop(0, S)
    def _(b):
        full = dot_nn(place[0], qf[b]) + dot_nn(place[1], qf[S + b])
        cot_ref[:, pl.ds(pl.multiple_of(b * ES, ES), ES)] = full.astype(BF16)

    stores[0].start()

    @pl.loop(0, 2)
    def _(m):
        @pl.loop(1, S)
        def _(k):
            arrived(g_c.at[m * S + lax.rem(cc(m) + S - k, S)], s4.at[m * S + k])

    for m, gain in ((0, gt_ref), (1, gi_ref)):
        for half in range(2):
            total = g_c[m * S + half]
            for k in range(half + 2, S, 2):
                total = total + g_c[m * S + k]
            for g in range(S // 2):
                for i in range(GR):
                    zq, off = (i * 128) // CH, (i * 128) % CH
                    first = zq * S * CH + (half + 2 * g) * CH + off
                    at = slice(first, first + 128)
                    gain_ref[m, :, at] = total[g * GR + i:g * GR + i + 1, :] / gain[:, at]

    stores[4].start()
    stores[5].start()

    @pl.loop(0, 2)
    def _(m):
        own = ring_end(m * 2 + group(m))
        arrived(dw_xr.at[m], e3.at[m])
        dw_end[m] = own + dw_xr[m].astype(F32)

    stores[2].start()
    stores[3].start()

    sent(w.at[pl.ds(0, 4)], send.at[1])
    sent(gs.at[pl.ds(0, 2 * (S - 1))], send.at[2])
    sent(gall.at[pl.ds(0, 2 * S)], send.at[3])
    sent(xs.at[pl.ds(0, 2)], send.at[4])
    sent(xall.at[pl.ds(0, 8)], send.at[5])
    sent(xall.at[pl.ds(0, 4)], send.at[0])
    sent(dw_own.at[pl.ds(0, 4)], send.at[6])
    sent(qp.at[pl.ds(0, 2 * S)], send.at[7])
    sent(dp.at[pl.ds(0, 8)], send.at[8])
    sent(dp.at[pl.ds(0, 4)], send.at[22])
    sent(g_core.at[pl.ds(0, 2)], send.at[9])
    sent(dw_peer, send.at[10])
    if H > 1:
        sent(ring.at[pl.ds(0, 8 * (H - 1))], send.at[11])
    sent(g_b.at[pl.ds(0, 2 * (S - 1))], send.at[12])
    sent(g_z.at[pl.ds(0, 2 * (NZ - 1))], send.at[13])
    sent(g_c.at[pl.ds(0, 2 * (S - 1))], send.at[14])
    sent(qp.at[pl.ds(0, 2 * (S - 1))], send.at[15])
    sent(dp.at[pl.ds(0, 2)], send.at[16])
    sent(dw_x, send.at[17])
    if H > 1:
        sent(ring.at[pl.ds(0, 8 * (H - 1))], send.at[18])
    sent(dw_own.at[pl.ds(0, 4)], send.at[19])
    sent(dw_x, send.at[20])
    for store in stores:
        store.wait()


def hand_on(*refs):
    came, gone = refs[-2:]
    count = (len(refs) - 2) // 3
    loads, stores = [], []
    for i in range(count):
        rows = refs[i].shape[0]
        step = max(rows // 4, 1)
        for first in range(0, rows, step):
            at, sem = pl.ds(first, step), len(loads)
            held = refs[2 * count + i].at[at]
            loads.append(pltpu.make_async_copy(refs[i].at[at], held, came.at[sem]))
            stores.append(pltpu.make_async_copy(held, refs[count + i].at[at], gone.at[sem]))
    for load in loads:
        load.start()
    for load, store in zip(loads, stores):
        load.wait()
        store.start()
    for store in stores:
        store.wait()


def solution(mesh):
    ZL, S = mesh.shape["dp"], mesh.shape["text"] // 2
    NZ = 2 * ZL
    H = NZ // 2

    def shards(tokens, modality, gain_text, gain_image, text_weight, image_weight, cotangent):
        T, D = tokens.shape
        E = cotangent.shape[1]
        R = -(-min(CAP, T) // 16) * 16
        DS, ES = D // S, E // S
        CH = DS // ZL
        WR, WC = CH // 2, ES // 2
        GR = DS // 128
        vmem = pl.BlockSpec(memory_space=pltpu.VMEM)
        dma = pltpu.SemaphoreType.DMA
        dims = (S, ZL, T, R, DS, ES)
        anywhere = pl.BlockSpec(memory_space=pl.ANY)
        modality, gain_text, gain_image = (
            modality.reshape(1, T), gain_text.reshape(1, D), gain_image.reshape(1, D)
        )
        shapes = (
            jax.ShapeDtypeStruct((T, E), BF16),
            jax.ShapeDtypeStruct((T, D), BF16),
            jax.ShapeDtypeStruct((WR, WC), F32),
            jax.ShapeDtypeStruct((WR, WC), F32),
            jax.ShapeDtypeStruct((1, D), F32),
            jax.ShapeDtypeStruct((1, D), F32),
        )
        parts = pl.pallas_call(
            functools.partial(layer, dims),
            out_shape=shapes,
            in_specs=[vmem] * 3 + [anywhere] * 4,
            out_specs=(anywhere,) * 6,
            scratch_shapes=[
                pltpu.VMEM((T, D), BF16),
                pltpu.VMEM((T, E), BF16),
                pltpu.VMEM((2 * R, T), BF16),
                pltpu.VMEM((2, T, R), BF16),
                pltpu.VMEM((T, 1), F32),
                pltpu.VMEM((T, 1), F32),
                pltpu.VMEM((2 * CH, ES), F32),
                pltpu.VMEM((T, D), F32),
                pltpu.VMEM((4, 1, DS), F32),
                pltpu.VMEM((4, 2, R, DS), BF16),
                pltpu.VMEM((2 * S, R, ES), BF16),
                pltpu.VMEM((4 * S, 2, R, DS), BF16),
                pltpu.VMEM((4 * S, R, ES), BF16),
                pltpu.VMEM((8, DS, WC), BF16),
                pltpu.VMEM((4 * S, R, ES), BF16),
                pltpu.VMEM((4 * S, 2, R, DS), BF16),
                pltpu.VMEM((2 * S, R, ES), BF16),
                pltpu.VMEM((8, R, DS), BF16),
                pltpu.VMEM((8, 2, R, DS), BF16),
                pltpu.VMEM((2 * S, R, ES), BF16),
                pltpu.VMEM((4, 2, R, DS), BF16),
                pltpu.VMEM((4 * NZ, WR, WC), BF16),
                pltpu.VMEM((4 * NZ, WR, WC), BF16),
                pltpu.VMEM((4 * NZ, WR, WC), BF16),
                pltpu.VMEM((8 * H, WR, WC), BF16),
                pltpu.VMEM((2, WR, WC), BF16),
                pltpu.VMEM((2, WR, WC), BF16),
                pltpu.VMEM((2, WR, WC), F32),
                pltpu.VMEM((4, 2 * GR, 128), F32),
                pltpu.VMEM((2 * S, 2 * GR, 128), F32),
                pltpu.VMEM((2 * NZ, 2 * GR, 128), F32),
                pltpu.VMEM((2 * S, 2 * GR, 128), F32),
                pltpu.VMEM((2, 1, D), F32),
                dma((6,)),
                dma((23,)),
                dma((2,)),
                dma((16,)),
                dma((2 * S,)),
                dma((2 * S,)),
                dma((2,)),
                dma((8 * H,)),
                dma((4 * NZ,)),
                dma((2 * S,)),
                dma((2 * S,)),
                dma((4,)),
                dma((8,)),
                dma((2,)),
                dma((4 * NZ,)),
                dma((8 * H,)),
                dma((2,)),
                dma((2,)),
                dma((2 * S,)),
                dma((2 * NZ,)),
                dma((2 * S,)),
            ],
            compiler_params=pltpu.CompilerParams(
                collective_id=0, has_side_effects=True, vmem_limit_bytes=60 * 2**20
            ),
        )(modality, gain_text, gain_image, tokens, cotangent, text_weight, image_weight)
        outs = pl.pallas_call(
            hand_on,
            out_shape=shapes,
            in_specs=[anywhere] * 6,
            out_specs=(anywhere,) * 6,
            scratch_shapes=[pltpu.VMEM(a.shape, a.dtype) for a in shapes] + [dma((18,)), dma((18,))],
            compiler_params=pltpu.CompilerParams(vmem_limit_bytes=60 * 2**20),
        )(*parts)
        return (*outs[:4], outs[4].reshape(D), outs[5].reshape(D))

    rows = P(("dp", "text", "image"), None)
    text_at, image_at = P(("dp", "image"), "text"), P(("dp", "text"), "image")
    return jax.shard_map(
        shards,
        mesh=mesh,
        in_specs=(rows, P(("dp", "text", "image")), P(), P(), text_at, image_at, rows),
        out_specs=(rows, rows, text_at, image_at, P(), P()),
        check_vma=False,
    )
```
